32 devices in a mesh: gx: 2 (over core), gy: 4 (over y, x), gz: 4 (over z).
Axes of the slice: x: 2, y: 2, z: 4, core: 2. Of those that a mesh axis runs over, the one named last changes fastest.
Arguments:
- latent: bfloat16 [16, 64, 64, 256], P('gx', 'gy', 'gz'), may hold values from -700 to 700
- norm_gain: float32 [256], replicated, may hold values from 0.5 to 1.5
- norm_shift: float32 [256], replicated, may hold values from -3 to 3
- w_qkv: bfloat16 [256, 768], replicated, may hold values from -40 to 40
- w_out: bfloat16 [256, 256], replicated, may hold values from -0.375 to 0.375
- b_out: float32 [256], replicated, may hold values from -3 to 3
- depth_limit: int32 [4, 16, 16], P('gx', 'gy', 'gz'), may hold values from 0 to 1
Outputs:
- attended_out: bfloat16 [16, 64, 64, 256], P('gx', 'gy', 'gz')
The draws below stay inside these ranges and needn't reach their ends.
All inputs are finite; a program needn't handle non-finite values.
Results may differ from the reference program's by a relative error of at most 0.038.
Values may be sent and summed in bfloat16 or wider, within the bound.
A program may use at most 128 MiB of HBM per device.

```python
import math
import jax
import jax.numpy as jnp
import numpy as np
from jax import lax

D = 256
HEADS = 8
GROUPS = 32
NX = 16
NY = 64
NZ = 64


def draw_latent(key, part):
    key = jax.random.fold_in(key, 1)
    first = jax.random.fold_in(key, 0)
    second = jax.random.fold_in(key, 1)
    fourth = jax.random.fold_in(key, 3)
    pos_x = jnp.arange(NX, dtype=jnp.float32) / NX
    pos_y = jnp.arange(NY, dtype=jnp.float32) / NY
    pos_z = jnp.arange(NZ, dtype=jnp.float32) / NZ
    rising = jnp.exp(math.log(3.0) * (pos_x[:, None, None] + pos_y[None, :, None] + pos_z[None, None, :]))[..., None] / 5.0
    cell_scale = jnp.exp(jax.random.uniform(second, (NX, NY, NZ, 1), jnp.float32) * math.log(10.0))
    common = jnp.clip(jax.random.normal(fourth, (D,), jnp.float32), -2.0, 2.0)
    base = jnp.clip(jax.random.normal(first, (NX, NY, NZ, D), jnp.float32), -6.0, 6.0) + common
    return (base * cell_scale * rising).astype(jnp.bfloat16)


def draw_w_qkv(key, part):
    key = jax.random.fold_in(key, 2)
    first = jax.random.fold_in(key, 0)
    base = jnp.clip(jax.random.normal(first, (D, 3 * D), jnp.float32), -6.0, 6.0) / math.sqrt(D)
    return base.astype(jnp.bfloat16)


def touch_ends(values, key, low, largest):
    shape = values.shape
    spot = [jax.random.randint(jax.random.fold_in(key, axis), (), 0, shape[axis]) for axis in range(len(shape))]
    values = values.at[tuple(spot)].set(low)
    longest = shape.index(max(shape))
    spot[longest] = (spot[longest] + 1) % shape[longest]
    return values.at[tuple(spot)].set(largest)


def gaussian(key, extent, scale, reach, held_as=jnp.bfloat16):
    values = jax.random.normal(key, extent, jnp.float32) * scale
    return jnp.minimum(jnp.maximum(values, -reach), reach).astype(held_as)


def setup_inputs(seed: int = 0) -> dict:
    arg_keys = jax.random.split(jax.random.key(seed), 8)
    latent = draw_latent(jax.random.fold_in(arg_keys[7], 71), 0)
    norm_gain = jnp.clip(1.0 + 0.1 * jax.random.normal(arg_keys[1], (D,), jnp.float32), 0.5, 1.5)
    norm_shift = gaussian(arg_keys[2], (D,), 0.5, 3.0, jnp.float32)
    w_qkv = draw_w_qkv(jax.random.fold_in(arg_keys[7], 71), 0)
    w_out = gaussian(arg_keys[4], (D, D), D ** -0.5, 0.375)
    b_out = gaussian(arg_keys[5], (D,), 0.5, 3.0, jnp.float32)
    depth_limit = touch_ends(jax.random.randint(arg_keys[6], (NX // 4, NY // 4, NZ // 4), 0, 2), jax.random.fold_in(arg_keys[6], 1), 0, 1).astype(jnp.int32)
    return {"latent": latent, "norm_gain": norm_gain, "norm_shift": norm_shift, "w_qkv": w_qkv, "w_out": w_out, "b_out": b_out, "depth_limit": depth_limit}


neighbour_offsets = [(first, second, third) for first in range(3) for second in range(3) for third in range(3)]

def to_blocks(field):
    size_x, size_y, size_z, chans = field.shape
    shaped = field.reshape(size_x // 4, 4, size_y // 4, 4, size_z // 4, 4, chans)
    return shaped.transpose(0, 2, 4, 1, 3, 5, 6).reshape(size_x // 4, size_y // 4, size_z // 4, 64, chans)

def from_blocks(blocks):
    count_x, count_y, count_z, cells, chans = blocks.shape
    shaped = blocks.reshape(count_x, count_y, count_z, 4, 4, 4, chans)
    return shaped.transpose(0, 3, 1, 4, 2, 5, 6).reshape(count_x * 4, count_y * 4, count_z * 4, chans)

def valid_table(limit, start_x, start_y, start_z, total_x, total_y, total_z):
    table = jnp.asarray(np.array(neighbour_offsets, dtype=np.int32) - 1)
    index_x = start_x + jnp.arange(limit.shape[0], dtype=jnp.int32)
    index_y = start_y + jnp.arange(limit.shape[1], dtype=jnp.int32)
    index_z = start_z + jnp.arange(limit.shape[2], dtype=jnp.int32)
    key_x = index_x[:, None] + table[None, :, 0]
    key_y = index_y[:, None] + table[None, :, 1]
    key_z = index_z[:, None] + table[None, :, 2]
    inside_x = (key_x >= 0) & (key_x < total_x)
    inside_y = (key_y >= 0) & (key_y < total_y)
    inside_z = (key_z >= 0) & (key_z < total_z)
    depth_ok = jnp.abs(table[:, 2])[None, None, None, :] <= limit[..., None]
    return inside_x[:, None, None, :] & inside_y[None, :, None, :] & inside_z[None, None, :, :] & depth_ok

def attend_span(query_blocks, region, valid, heads):
    depth = query_blocks.shape[1]
    width = query_blocks.shape[-1]
    head_dim = width // heads
    pieces = [region[first, second:second + 2, third:third + depth] for first, second, third in neighbour_offsets]
    keyvals = jnp.stack(pieces, axis=2).reshape(2, depth, 27 * 64, 2 * width)
    keys = keyvals[..., :width].reshape(2, depth, 27 * 64, heads, head_dim).astype(jnp.float32)
    values = keyvals[..., width:].reshape(2, depth, 27 * 64, heads, head_dim).astype(jnp.float32)
    queries = query_blocks.reshape(2, depth, 64, heads, head_dim).astype(jnp.float32)
    scores = jnp.einsum('abqhd,abkhd->abhqk', queries, keys) * head_dim ** (-0.5)
    allowed = jnp.repeat(valid, 64, axis=-1)
    scores = jnp.where(allowed[:, :, None, None, :], scores, jnp.float32(-1e+30))
    top = lax.optimization_barrier(jnp.max(scores, axis=-1, keepdims=True))
    expd = jnp.exp(scores - top)
    weights = (expd / lax.optimization_barrier(jnp.sum(expd, axis=-1, keepdims=True))).astype(jnp.bfloat16)
    mixed = jnp.einsum('abhqk,abkhd->abqhd', weights.astype(jnp.float32), values)
    return mixed.astype(jnp.bfloat16).reshape(2, depth, 64, width)

def attend_all(query_blocks, kv_blocks, valid, heads):
    count_x, count_y, count_z = query_blocks.shape[:3]
    width = query_blocks.shape[-1]
    pairs = count_y // 2
    zero = jnp.zeros((), jnp.int32)

    def one_span(index):
        block_x = (index // pairs).astype(jnp.int32)
        block_y = (index % pairs * 2).astype(jnp.int32)
        query_part = lax.dynamic_slice(query_blocks, (block_x, block_y, zero, zero, zero), (1, 2, count_z, 64, width))[0]
        region = lax.dynamic_slice(kv_blocks, (block_x, block_y, zero, zero, zero), (3, 4, count_z + 2, 64, 2 * width))
        valid_part = lax.dynamic_slice(valid, (block_x, block_y, zero, zero), (1, 2, count_z, 27))[0]
        return attend_span(query_part, region, valid_part, heads)
    result = lax.map(one_span, jnp.arange(count_x * pairs, dtype=jnp.int32))
    return result.reshape(count_x, count_y, count_z, 64, width)

def reference(latent, norm_gain, norm_shift, w_qkv, w_out, b_out, depth_limit):
    size_x, size_y, size_z, width = latent.shape
    grouped = latent.astype(jnp.float32).reshape(-1, GROUPS, width // GROUPS)
    count = grouped.shape[0] * grouped.shape[2]
    mean = lax.optimization_barrier(jnp.sum(grouped, axis=(0, 2))) / count
    centred = grouped - mean[None, :, None]
    var = lax.optimization_barrier(jnp.sum(centred * centred, axis=(0, 2))) / count
    normed = (centred * lax.rsqrt(var + 1e-06)[None, :, None]).reshape(size_x, size_y, size_z, width)
    normed = (normed * norm_gain + norm_shift).astype(jnp.bfloat16)
    qkv = jnp.dot(normed.reshape(-1, width), w_qkv, preferred_element_type=jnp.float32).astype(jnp.bfloat16)
    queries = qkv[:, :width].reshape(size_x, size_y, size_z, width)
    keyvals = qkv[:, width:].reshape(size_x, size_y, size_z, 2 * width)
    padded = jnp.pad(keyvals, ((4, 4), (4, 4), (4, 4), (0, 0)))
    valid = valid_table(depth_limit, 0, 0, 0, size_x // 4, size_y // 4, size_z // 4)
    mixed = from_blocks(attend_all(to_blocks(queries), to_blocks(padded), valid, HEADS))
    output = jnp.dot(mixed.reshape(-1, width), w_out, preferred_element_type=jnp.float32) + b_out
    return output.astype(jnp.bfloat16).reshape(size_x, size_y, size_z, width)
```

```python
import functools
import math

import jax
import jax.numpy as jnp
from jax import lax
from jax.experimental import pallas as pl
from jax.experimental.pallas import tpu as pltpu
from jax.sharding import PartitionSpec as P

HEADS = 8
GROUPS = 32
CELLS = 64
CHUNK = 4
LOW = -1e30


def halo(blocks, sides):
    for axis, dim in sides:
        count = lax.axis_size(axis)
        ends = count - 1
        head = lax.slice_in_dim(blocks, 0, 1, axis=dim)
        tail = lax.slice_in_dim(blocks, blocks.shape[dim] - 1, blocks.shape[dim], axis=dim)
        blocks = jnp.concatenate(
            [
                lax.ppermute(tail, axis, [(i, i + 1) for i in range(ends)]),
                blocks,
                lax.ppermute(head, axis, [(i + 1, i) for i in range(ends)]),
            ],
            axis=dim,
        )
    return blocks


def to_blocks(field):
    size_x, size_y, size_z, chans = field.shape
    shaped = field.reshape(size_x // 4, 4, size_y // 4, 4, size_z // 4, 4, chans)
    return shaped.transpose(0, 2, 4, 1, 3, 5, 6).reshape(
        size_x // 4, size_y // 4, size_z // 4, CELLS, chans
    )


def attend_kernel(
    counts, place_ref, limit_ref, x_ref, mean_ref, gain_ref, shift_ref, wqkv_ref, wout_ref,
    bout_ref, out_ref, k_ref, v_ref, s_ref, top_ref, sum_ref, acc_ref, mix_ref,
):
    count_x, count_y, count_z = counts
    pad_y, pad_z = count_y + 2, count_z + 2
    width = x_ref.shape[1]
    head_dim = width // HEADS
    rows = HEADS * CELLS
    keys = CHUNK * CELLS
    factor = head_dim ** (-0.5) * math.log2(math.e)

    def normed(x):
        scaled = (x.astype(jnp.float32) - mean_ref[...]) * gain_ref[...]
        return (scaled + shift_ref[...]).astype(jnp.bfloat16)

    def low(axis, index):
        return jnp.where(place_ref[axis] + index > 0, index, index + 1)

    def high(axis, index):
        return jnp.where(place_ref[axis] + index + 1 < place_ref[3 + axis], index + 2, index + 1)

    first_x, last_x = low(0, 0), high(0, count_x - 1)
    first_y, last_y = low(1, 0), high(1, count_y - 1)
    column = pad_z * CELLS

    def project(index, carry):
        index_x, index_y = index // pad_y, index % pad_y
        inside = (
            (index_x >= first_x) & (index_x <= last_x) & (index_y >= first_y) & (index_y <= last_y)
        )

        @pl.when(inside)
        def _():
            span = pl.ds(pl.multiple_of(index * column, column), column)
            cells = normed(x_ref[span, :])
            k_ref[span, :] = jnp.dot(
                cells, wqkv_ref[:, width : 2 * width], preferred_element_type=jnp.float32
            ).astype(jnp.bfloat16)
            v_ref[span, :] = jnp.dot(
                cells, wqkv_ref[:, 2 * width :], preferred_element_type=jnp.float32
            ).astype(jnp.bfloat16)

        return carry

    lax.fori_loop(0, (count_x + 2) * pad_y, project, 0)

    lane_head = lax.broadcasted_iota(jnp.int32, (CELLS, width), 1) // head_dim

    def one_block(block_x, block_y, block_z):
        limit = limit_ref[(block_x * count_y + block_y) * count_z + block_z]
        lo_x, hi_x = low(0, block_x), high(0, block_x)
        lo_y, hi_y = low(1, block_y), high(1, block_y)
        lo_z = jnp.where(limit > 0, low(2, block_z), block_z + 1)
        hi_z = jnp.where(limit > 0, high(2, block_z), block_z + 1)
        total = (hi_x - lo_x + 1) * (hi_y - lo_y + 1) * (hi_z - lo_z + 1)
        full = total // CHUNK
        chunks = (total + CHUNK - 1) // CHUNK
        start = (lo_x, lo_y, lo_z)

        def flat(at_x, at_y, at_z):
            return (at_x * pad_y + at_y) * pad_z + at_z

        def gather(ref, at):
            pieces = []
            at_x, at_y, at_z = at
            for _ in range(CHUNK):
                index = pl.multiple_of(flat(at_x, at_y, at_z) * CELLS, CELLS)
                pieces.append(ref[pl.ds(index, CELLS), :])
                turn_z = at_z == hi_z
                at_z = jnp.where(turn_z, lo_z, at_z + 1)
                turn_y = turn_z & (at_y == hi_y)
                at_y = jnp.where(turn_y, lo_y, jnp.where(turn_z, at_y + 1, at_y))
                at_x = jnp.where(turn_y, jnp.minimum(at_x + 1, hi_x), at_x)
            return jnp.concatenate(pieces, axis=0), (at_x, at_y, at_z)

        own = pl.multiple_of(flat(block_x + 1, block_y + 1, block_z + 1) * CELLS, CELLS)
        query = jnp.dot(
            normed(x_ref[pl.ds(own, CELLS), :]),
            wqkv_ref[:, :width],
            preferred_element_type=jnp.float32,
        )
        stacked = jnp.concatenate(
            [jnp.where(lane_head == head, query, 0.0).astype(jnp.bfloat16) for head in range(HEADS)],
            axis=0,
        )
        top_ref[...] = jnp.full_like(top_ref, LOW)

        def score(index, at, masked):
            chunk, at = gather(k_ref, at)
            scores = lax.dot_general(
                stacked, chunk, (((1,), (1,)), ((), ())), preferred_element_type=jnp.float32
            )
            if masked:
                lane = lax.broadcasted_iota(jnp.int32, (1, keys), 1) + index * keys
                scores = jnp.where(lane < total * CELLS, scores, LOW)
            s_ref[index] = scores
            best = scores[:, :128]
            for part in range(1, keys // 128):
                best = jnp.maximum(best, scores[:, part * 128 : (part + 1) * 128])
            top_ref[...] = jnp.maximum(top_ref[...], best)
            return at

        at = lax.fori_loop(0, full, functools.partial(score, masked=False), start)

        @pl.when(chunks > full)
        def _():
            score(full, at, True)

        top = jnp.max(top_ref[...], axis=1, keepdims=True) * factor
        top_ref[...] = jnp.broadcast_to(top, top_ref.shape)
        sum_ref[...] = jnp.zeros_like(sum_ref)
        acc_ref[...] = jnp.zeros_like(acc_ref)

        def mix(index, at):
            chunk, at = gather(v_ref, at)
            weights = []
            added = None
            for part in range(keys // 128):
                scores = s_ref[index, :, part * 128 : (part + 1) * 128]
                weight = jnp.exp2(scores * factor - top_ref[...])
                added = weight if added is None else added + weight
                weights.append(weight.astype(jnp.bfloat16))
            sum_ref[...] += added
            acc_ref[...] += jnp.dot(
                jnp.concatenate(weights, axis=1), chunk, preferred_element_type=jnp.float32
            )
            return at

        lax.fori_loop(0, chunks, mix, start)
        share = 1.0 / jnp.sum(sum_ref[...], axis=1, keepdims=True)
        mixed = jnp.zeros((CELLS, width), jnp.float32)
        for head in range(HEADS):
            part = slice(head * CELLS, (head + 1) * CELLS)
            mixed = jnp.where(lane_head == head, acc_ref[part, :] * share[part], mixed)
        return mixed.astype(jnp.bfloat16)

    slab = count_z * CELLS
    natural = lax.broadcasted_iota(jnp.int32, (slab, slab), 0)
    blocked = lax.broadcasted_iota(jnp.int32, (slab, slab), 1)
    depth = natural % (count_z * 4)
    moved = depth // 4 * CELLS + natural // (count_z * 4) * 4 + depth % 4
    order = (moved == blocked).astype(jnp.bfloat16)

    def one_column(index, carry):
        block_x, block_y = index // count_y, index % count_y

        def one_depth(block_z, carry):
            span = pl.ds(pl.multiple_of(block_z * CELLS, CELLS), CELLS)
            mix_ref[span, :] = one_block(block_x, block_y, block_z)
            return carry

        lax.fori_loop(0, count_z, one_depth, 0)
        cells = jnp.dot(order, mix_ref[...], preferred_element_type=jnp.float32)
        result = jnp.dot(
            cells.astype(jnp.bfloat16), wout_ref[...], preferred_element_type=jnp.float32
        )
        result = (result + bout_ref[...]).astype(jnp.bfloat16)
        out_ref[pl.ds(block_x * 4, 4), pl.ds(block_y * 4, 4), :, :] = result.reshape(
            4, 4, count_z * 4, width
        )
        return carry

    lax.fori_loop(0, count_x * count_y, one_column, 0)


def attend(place, limit, padded, mean, gain, shift, w_qkv, w_out, b_out):
    counts = limit.shape
    width = padded.shape[-1]
    flat = padded.reshape(-1, width)
    rows = HEADS * CELLS
    most = -(-27 // CHUNK)
    smem = pl.BlockSpec(memory_space=pltpu.SMEM)
    vmem = pl.BlockSpec(memory_space=pltpu.VMEM)
    return pl.pallas_call(
        functools.partial(attend_kernel, counts),
        out_shape=jax.ShapeDtypeStruct(
            (counts[0] * 4, counts[1] * 4, counts[2] * 4, width), jnp.bfloat16
        ),
        in_specs=[smem, smem] + [vmem] * 7,
        out_specs=vmem,
        scratch_shapes=[
            pltpu.VMEM(flat.shape, jnp.bfloat16),
            pltpu.VMEM(flat.shape, jnp.bfloat16),
            pltpu.VMEM((most, rows, CHUNK * CELLS), jnp.float32),
            pltpu.VMEM((rows, 128), jnp.float32),
            pltpu.VMEM((rows, 128), jnp.float32),
            pltpu.VMEM((rows, width), jnp.float32),
            pltpu.VMEM((counts[2] * CELLS, width), jnp.bfloat16),
        ],
        compiler_params=pltpu.CompilerParams(vmem_limit_bytes=48 * 2**20),
        cost_estimate=pl.CostEstimate(
            flops=30 * 10**9, bytes_accessed=7 * 10**6, transcendentals=28 * 10**6
        ),
    )(place, limit.reshape(-1), flat, mean, gain, shift, w_qkv, w_out, b_out)


def on_device(latent, norm_gain, norm_shift, w_qkv, w_out, b_out, depth_limit):
    width = latent.shape[-1]
    per = width // GROUPS
    axes = ("gx", "gy", "gz")
    grouped = latent.astype(jnp.float32).reshape(-1, GROUPS, per)
    count = grouped.shape[0] * per
    mean_here = jnp.sum(grouped, axis=(0, 2)) / count
    centred = grouped - mean_here[None, :, None]
    square_here = jnp.sum(centred * centred, axis=(0, 2)) / count
    parts = lax.all_gather(jnp.stack([mean_here, square_here]), axes)
    mean = jnp.mean(parts[:, 0], axis=0)
    var = jnp.mean(parts[:, 1] + (parts[:, 0] - mean) ** 2, axis=0)
    gain = jnp.repeat(lax.rsqrt(var + 1e-06), per) * norm_gain
    padded = halo(to_blocks(latent), (("gy", 1), ("gz", 2), ("gx", 0)))
    counts = depth_limit.shape
    place = jnp.stack(
        [lax.axis_index(axis) * n for axis, n in zip(axes, counts)]
        + [jnp.int32(lax.axis_size(axis) * n) for axis, n in zip(axes, counts)]
    ).astype(jnp.int32)
    return attend(
        place, depth_limit, padded, jnp.repeat(mean, per)[None], gain[None], norm_shift[None],
        w_qkv, w_out, b_out[None],
    )


def solution(mesh):
    placed = (P("gx", "gy", "gz", None), P(), P(), P(), P(), P(), P("gx", "gy", "gz"))
    return jax.shard_map(
        on_device, mesh=mesh, in_specs=placed, out_specs=P("gx", "gy", "gz", None), check_vma=False
    )
```

```python
import functools
import math

import jax
import jax.numpy as jnp
from jax import lax
from jax.experimental import pallas as pl
from jax.experimental.pallas import tpu as pltpu
from jax.sharding import PartitionSpec as P

HEADS = 8
GROUPS = 32
CELLS = 64
CHUNK = 4
LOW = -1e30


def cell_order(slab, inverse):
    natural = lax.broadcasted_iota(jnp.int32, (slab, slab), 0 if inverse else 1)
    blocked = lax.broadcasted_iota(jnp.int32, (slab, slab), 1 if inverse else 0)
    depth = blocked // CELLS * 4 + blocked % 4
    found = blocked % CELLS // 4 * (slab // 16) + depth
    return (found == natural).astype(jnp.bfloat16)


def exchange_kernel(counts, sizes, latent_ref, pad_ref, stats_ref, here, there, *sems):
    send_sem, recv_sem, stat_send, stat_recv = sems
    count_x, count_y, count_z = counts
    width = latent_ref.shape[-1]
    slab = count_z * CELLS
    axes = ("gx", "gy", "gz")
    me = [lax.axis_index(axis) for axis in axes]

    def at(axis, position):
        return tuple(position if n == axis else me[n] for n in range(3))

    barrier = pltpu.get_barrier_semaphore()
    for axis in range(3):
        for step in range(1, sizes[axis]):
            pl.semaphore_signal(
                barrier, inc=1, device_id=at(axis, lax.rem(me[axis] + step, sizes[axis])),
                device_id_type=pl.DeviceIdType.MESH,
            )

    order = cell_order(slab, False)
    for block_x in range(count_x):
        for block_y in range(count_y):
            cells = latent_ref[
                block_x * 4 : block_x * 4 + 4, block_y * 4 : block_y * 4 + 4, :, :
            ].reshape(slab, width)
            blocks = jnp.dot(order, cells, preferred_element_type=jnp.float32)
            pad_ref[1 + block_x, 1 + block_y, 1 : 1 + count_z] = (
                blocks.astype(jnp.bfloat16).reshape(count_z, CELLS, width)
            )
    pl.semaphore_wait(barrier, sum(sizes) - 3)

    def has(axis, step):
        return me[axis] > 0 if step < 0 else me[axis] < sizes[axis] - 1

    copies = []

    def layer(axis, side, spans):
        count = counts[axis]
        source = list(spans)
        target = list(spans)
        source[axis] = pl.ds(1 if side < 0 else count, 1)
        target[axis] = pl.ds(count + 1 if side < 0 else 0, 1)
        return tuple(source), tuple(target)

    def send(axis, side, spans, given=None):
        number = len(copies)
        source, target = layer(axis, side, spans)
        to = me[axis] + side
        copy = pltpu.make_async_remote_copy(
            src_ref=pad_ref.at[source],
            dst_ref=pad_ref.at[target],
            send_sem=send_sem.at[number],
            recv_sem=recv_sem.at[number],
            device_id=at(axis, to),
            device_id_type=pl.DeviceIdType.MESH,
        )
        leaves, comes = has(axis, side), has(axis, -side)
        if given is not None:
            leaves, comes = leaves & given, comes & given
        copies.append((copy, leaves, comes))

        @pl.when(leaves)
        def _():
            copy.start()

        return number

    def received(number):
        copy, _, comes = copies[number]

        @pl.when(comes)
        def _():
            copy.wait_recv()

    inner = [pl.ds(1, count) for count in counts]
    sides = (-1, 1)
    face_y = [send(1, side, inner) for side in sides]
    face_z = [send(2, side, inner) for side in sides]
    face_x = [send(0, side, inner) for side in sides]

    cells = latent_ref[...].reshape(-1, width).astype(jnp.float32)
    count = cells.shape[0]
    mean = jnp.sum(cells, axis=0, keepdims=True) / count
    centred = cells - mean
    var = jnp.sum(centred * centred, axis=0, keepdims=True) / count

    first = {0: 0, 1: sizes[0] - 1, 2: sizes[0] + sizes[1] - 2}

    def stat_copies(axis):
        found = []
        for step in range(1, sizes[axis]):
            slot = first[axis] + step - 1
            found.append(
                pltpu.make_async_remote_copy(
                    src_ref=here.at[axis],
                    dst_ref=there.at[slot],
                    send_sem=stat_send.at[slot],
                    recv_sem=stat_recv.at[slot],
                    device_id=at(axis, lax.rem(me[axis] + step, sizes[axis])),
                    device_id_type=pl.DeviceIdType.MESH,
                )
            )
        return found

    def stat_start(axis, mean, var):
        here[axis, 0:1, :] = mean
        here[axis, 1:2, :] = var
        found = stat_copies(axis)
        for copy in found:
            copy.start()
        return found

    def stat_end(axis, found, mean, var):
        for copy in found:
            copy.wait()
        means, variances = [mean], [var]
        for step in range(1, sizes[axis]):
            slot = first[axis] + step - 1
            means.append(there[slot, 0:1, :])
            variances.append(there[slot, 1:2, :])
        mean = sum(means) / sizes[axis]
        spread = [(part - mean) * (part - mean) for part in means]
        return mean, (sum(variances) + sum(spread)) / sizes[axis]

    found = stat_start(0, mean, var)
    mean, var = stat_end(0, found, mean, var)
    found = stat_start(1, mean, var)

    outer_y = [pl.ds(0, 1), pl.ds(count_y + 1, 1)]
    edge_z = []
    for number, side in enumerate(sides):
        received(face_y[1 - number])
        spans = [inner[0], outer_y[number], inner[2]]
        edge_z += [send(2, way, spans, has(1, side)) for way in sides]
    mean, var = stat_end(1, found, mean, var)
    found = stat_start(2, mean, var)
    for number, side in enumerate(sides):
        spans = [inner[0], outer_y[number], inner[2]]
        face_x += [send(0, way, spans, has(1, side)) for way in sides]
    mean, var = stat_end(2, found, mean, var)
    stats_ref[...] = jnp.zeros_like(stats_ref)
    stats_ref[0:1, :] = mean
    stats_ref[1:2, :] = var
    outer_z = [pl.ds(0, 1), pl.ds(count_z + 1, 1)]
    for number, side in enumerate(sides):
        received(face_z[1 - number])
        spans = [inner[0], inner[1], outer_z[number]]
        face_x += [send(0, way, spans, has(2, side)) for way in sides]
    for number, side in enumerate(sides):
        for other, side_y in enumerate(sides):
            received(edge_z[other * 2 + 1 - number])
            spans = [inner[0], outer_y[other], outer_z[number]]
            face_x += [
                send(0, way, spans, has(2, side) & has(1, side_y)) for way in sides
            ]
    for number in face_x:
        received(number)
    for copy, leaves, _ in copies:

        @pl.when(leaves)
        def _(copy=copy):
            copy.wait_send()


def exchange(latent, counts):
    width = latent.shape[-1]
    sizes = tuple(lax.axis_size(axis) for axis in ("gx", "gy", "gz"))
    partners = sum(sizes) - 3
    vmem = pl.BlockSpec(memory_space=pltpu.VMEM)
    padded = tuple(count + 2 for count in counts) + (CELLS, width)
    copies = 2 * (1 + 1 + 1 + 2 + 2 + 2 + 4)
    return pl.pallas_call(
        functools.partial(exchange_kernel, counts, sizes),
        out_shape=(
            jax.ShapeDtypeStruct(padded, jnp.bfloat16),
            jax.ShapeDtypeStruct((8, width), jnp.float32),
        ),
        in_specs=[vmem],
        out_specs=(vmem, vmem),
        scratch_shapes=[
            pltpu.VMEM((3, 8, width), jnp.float32),
            pltpu.VMEM((partners, 8, width), jnp.float32),
            pltpu.SemaphoreType.DMA((copies,)),
            pltpu.SemaphoreType.DMA((copies,)),
            pltpu.SemaphoreType.DMA((partners,)),
            pltpu.SemaphoreType.DMA((partners,)),
        ],
        compiler_params=pltpu.CompilerParams(
            collective_id=0, has_side_effects=True, vmem_limit_bytes=32 * 2**20
        ),
        cost_estimate=pl.CostEstimate(flops=10**9, bytes_accessed=6 * 10**6, transcendentals=0),
    )(latent)


def attend_kernel(
    counts, sizes, limit_ref, x_ref, stats_ref, scale_ref, shift_ref, wqkv_ref, wout_ref,
    bout_ref, out_ref, mean_ref, gain_ref, k_ref, v_ref, s_ref, top_ref, sum_ref, acc_ref, mix_ref,
):
    count_x, count_y, count_z = counts
    pad_y, pad_z = count_y + 2, count_z + 2
    width = x_ref.shape[1]
    head_dim = width // HEADS
    rows = HEADS * CELLS
    keys = CHUNK * CELLS
    factor = head_dim ** (-0.5) * math.log2(math.e)

    per = width // GROUPS
    group = lax.broadcasted_iota(jnp.int32, (width, width), 0) // per
    member = (group == lax.broadcasted_iota(jnp.int32, (width, width), 1) // per).astype(jnp.float32)

    def group_mean(row):
        whole = jnp.broadcast_to(row, (8, width))
        return jnp.dot(
            whole, member, precision=lax.Precision.HIGHEST, preferred_element_type=jnp.float32
        )[0:1] / per

    mean = group_mean(stats_ref[0:1, :])
    apart = stats_ref[0:1, :] - mean
    var = group_mean(stats_ref[1:2, :] + apart * apart)
    mean_ref[...] = mean
    gain_ref[...] = lax.rsqrt(var + 1e-06) * scale_ref[...]

    def normed(x):
        scaled = (x.astype(jnp.float32) - mean_ref[...]) * gain_ref[...]
        return (scaled + shift_ref[...]).astype(jnp.bfloat16)

    place = [lax.axis_index(axis) * n for axis, n in zip(("gx", "gy", "gz"), counts)]

    def low(axis, index):
        return jnp.where(place[axis] + index > 0, index, index + 1)

    def high(axis, index):
        return jnp.where(place[axis] + index + 1 < counts[axis] * sizes[axis], index + 2, index + 1)

    first_x, last_x = low(0, 0), high(0, count_x - 1)
    first_y, last_y = low(1, 0), high(1, count_y - 1)
    column = pad_z * CELLS

    def project(index, carry):
        index_x, index_y = index // pad_y, index % pad_y
        inside = (
            (index_x >= first_x) & (index_x <= last_x) & (index_y >= first_y) & (index_y <= last_y)
        )

        @pl.when(inside)
        def _():
            span = pl.ds(pl.multiple_of(index * column, column), column)
            cells = normed(x_ref[span, :])
            k_ref[span, :] = jnp.dot(
                cells, wqkv_ref[:, width : 2 * width], preferred_element_type=jnp.float32
            ).astype(jnp.bfloat16)
            v_ref[span, :] = jnp.dot(
                cells, wqkv_ref[:, 2 * width :], preferred_element_type=jnp.float32
            ).astype(jnp.bfloat16)

        return carry

    lax.fori_loop(0, (count_x + 2) * pad_y, project, 0)

    lane_head = lax.broadcasted_iota(jnp.int32, (CELLS, width), 1) // head_dim

    def one_block(block_x, block_y, block_z):
        limit = limit_ref[block_x, block_y, block_z]
        lo_x, hi_x = low(0, block_x), high(0, block_x)
        lo_y, hi_y = low(1, block_y), high(1, block_y)
        lo_z = jnp.where(limit > 0, low(2, block_z), block_z + 1)
        hi_z = jnp.where(limit > 0, high(2, block_z), block_z + 1)
        total = (hi_x - lo_x + 1) * (hi_y - lo_y + 1) * (hi_z - lo_z + 1)
        full = total // CHUNK
        chunks = (total + CHUNK - 1) // CHUNK
        start = (lo_x, lo_y, lo_z)

        def flat(at_x, at_y, at_z):
            return (at_x * pad_y + at_y) * pad_z + at_z

        def gather(ref, at):
            pieces = []
            at_x, at_y, at_z = at
            for _ in range(CHUNK):
                index = pl.multiple_of(flat(at_x, at_y, at_z) * CELLS, CELLS)
                pieces.append(ref[pl.ds(index, CELLS), :])
                turn_z = at_z == hi_z
                at_z = jnp.where(turn_z, lo_z, at_z + 1)
                turn_y = turn_z & (at_y == hi_y)
                at_y = jnp.where(turn_y, lo_y, jnp.where(turn_z, at_y + 1, at_y))
                at_x = jnp.where(turn_y, jnp.minimum(at_x + 1, hi_x), at_x)
            return jnp.concatenate(pieces, axis=0), (at_x, at_y, at_z)

        own = pl.multiple_of(flat(block_x + 1, block_y + 1, block_z + 1) * CELLS, CELLS)
        query = jnp.dot(
            normed(x_ref[pl.ds(own, CELLS), :]),
            wqkv_ref[:, :width],
            preferred_element_type=jnp.float32,
        )
        stacked = jnp.concatenate(
            [jnp.where(lane_head == head, query, 0.0).astype(jnp.bfloat16) for head in range(HEADS)],
            axis=0,
        )
        top_ref[...] = jnp.full_like(top_ref, LOW)

        def score(index, at, masked):
            chunk, at = gather(k_ref, at)
            scores = lax.dot_general(
                stacked, chunk, (((1,), (1,)), ((), ())), preferred_element_type=jnp.float32
            )
            if masked:
                lane = lax.broadcasted_iota(jnp.int32, (1, keys), 1) + index * keys
                scores = jnp.where(lane < total * CELLS, scores, LOW)
            s_ref[index] = scores
            best = scores[:, :128]
            for part in range(1, keys // 128):
                best = jnp.maximum(best, scores[:, part * 128 : (part + 1) * 128])
            top_ref[...] = jnp.maximum(top_ref[...], best)
            return at

        at = lax.fori_loop(0, full, functools.partial(score, masked=False), start)

        @pl.when(chunks > full)
        def _():
            score(full, at, True)

        top = jnp.max(top_ref[...], axis=1, keepdims=True) * factor
        top_ref[...] = jnp.broadcast_to(top, top_ref.shape)
        sum_ref[...] = jnp.zeros_like(sum_ref)
        acc_ref[...] = jnp.zeros_like(acc_ref)

        def mix(index, at):
            chunk, at = gather(v_ref, at)
            weights = []
            added = None
            for part in range(keys // 128):
                scores = s_ref[index, :, part * 128 : (part + 1) * 128]
                weight = jnp.exp2(scores * factor - top_ref[...])
                added = weight if added is None else added + weight
                weights.append(weight.astype(jnp.bfloat16))
            sum_ref[...] += added
            acc_ref[...] += jnp.dot(
                jnp.concatenate(weights, axis=1), chunk, preferred_element_type=jnp.float32
            )
            return at

        lax.fori_loop(0, chunks, mix, start)
        share = 1.0 / jnp.sum(sum_ref[...], axis=1, keepdims=True)
        mixed = jnp.zeros((CELLS, width), jnp.float32)
        for head in range(HEADS):
            part = slice(head * CELLS, (head + 1) * CELLS)
            mixed = jnp.where(lane_head == head, acc_ref[part, :] * share[part], mixed)
        return mixed.astype(jnp.bfloat16)

    slab = count_z * CELLS
    order = cell_order(slab, True)

    def one_column(index, carry):
        block_x, block_y = index // count_y, index % count_y

        def one_depth(block_z, carry):
            span = pl.ds(pl.multiple_of(block_z * CELLS, CELLS), CELLS)
            mix_ref[span, :] = one_block(block_x, block_y, block_z)
            return carry

        lax.fori_loop(0, count_z, one_depth, 0)
        cells = jnp.dot(order, mix_ref[...], preferred_element_type=jnp.float32)
        result = jnp.dot(
            cells.astype(jnp.bfloat16), wout_ref[...], preferred_element_type=jnp.float32
        )
        result = (result + bout_ref[...]).astype(jnp.bfloat16)
        out_ref[pl.ds(block_x * 4, 4), pl.ds(block_y * 4, 4), :, :] = result.reshape(
            4, 4, count_z * 4, width
        )
        return carry

    lax.fori_loop(0, count_x * count_y, one_column, 0)


def attend(limit, padded, stats, gain, shift, w_qkv, w_out, b_out):
    counts = limit.shape
    width = padded.shape[-1]
    flat = padded.reshape(-1, width)
    rows = HEADS * CELLS
    sizes = tuple(lax.axis_size(axis) for axis in ("gx", "gy", "gz"))
    most = -(-27 // CHUNK)
    smem = pl.BlockSpec(memory_space=pltpu.SMEM)
    vmem = pl.BlockSpec(memory_space=pltpu.VMEM)
    return pl.pallas_call(
        functools.partial(attend_kernel, counts, sizes),
        out_shape=jax.ShapeDtypeStruct(
            (counts[0] * 4, counts[1] * 4, counts[2] * 4, width), jnp.bfloat16
        ),
        in_specs=[smem] + [vmem] * 7,
        out_specs=vmem,
        scratch_shapes=[
            pltpu.VMEM((1, width), jnp.float32),
            pltpu.VMEM((1, width), jnp.float32),
            pltpu.VMEM(flat.shape, jnp.bfloat16),
            pltpu.VMEM(flat.shape, jnp.bfloat16),
            pltpu.VMEM((most, rows, CHUNK * CELLS), jnp.float32),
            pltpu.VMEM((rows, 128), jnp.float32),
            pltpu.VMEM((rows, 128), jnp.float32),
            pltpu.VMEM((rows, width), jnp.float32),
            pltpu.VMEM((counts[2] * CELLS, width), jnp.bfloat16),
        ],
        compiler_params=pltpu.CompilerParams(vmem_limit_bytes=48 * 2**20),
        cost_estimate=pl.CostEstimate(
            flops=30 * 10**9, bytes_accessed=7 * 10**6, transcendentals=28 * 10**6
        ),
    )(limit, flat, stats, gain, shift, w_qkv, w_out, b_out)


def on_device(latent, norm_gain, norm_shift, w_qkv, w_out, b_out, depth_limit):
    padded, stats = exchange(latent, depth_limit.shape)
    return attend(
        depth_limit, padded, stats, norm_gain[None], norm_shift[None], w_qkv, w_out, b_out[None]
    )


def solution(mesh):
    placed = (P("gx", "gy", "gz", None), P(), P(), P(), P(), P(), P("gx", "gy", "gz"))
    return jax.shard_map(
        on_device, mesh=mesh, in_specs=placed, out_specs=P("gx", "gy", "gz", None), check_vma=False
    )
```

```python
import functools
import math

import jax
import jax.numpy as jnp
from jax import lax
from jax.experimental import pallas as pl
from jax.experimental.pallas import tpu as pltpu
from jax.sharding import PartitionSpec as P

HEADS = 8
GROUPS = 32
CELLS = 64
CHUNK = 4
LOW = -1e30


def cell_order(slab, inverse):
    natural = lax.broadcasted_iota(jnp.int32, (slab, slab), 0 if inverse else 1)
    blocked = lax.broadcasted_iota(jnp.int32, (slab, slab), 1 if inverse else 0)
    depth = blocked // CELLS * 4 + blocked % 4
    found = blocked % CELLS // 4 * (slab // 16) + depth
    return (found == natural).astype(jnp.bfloat16)


def exchange_kernel(counts, sizes, latent_ref, pad_ref, stats_ref, here, there, *sems):
    send_sem, recv_sem, stat_send, stat_recv = sems
    count_x, count_y, count_z = counts
    width = latent_ref.shape[-1]
    slab = count_z * CELLS
    axes = ("gx", "gy", "gz")
    me = [lax.axis_index(axis) for axis in axes]

    def at(axis, position):
        return tuple(position if n == axis else me[n] for n in range(3))

    barrier = pltpu.get_barrier_semaphore()
    for axis in range(3):
        for step in range(1, sizes[axis]):
            pl.semaphore_signal(
                barrier, inc=1, device_id=at(axis, lax.rem(me[axis] + step, sizes[axis])),
                device_id_type=pl.DeviceIdType.MESH,
            )

    order = cell_order(slab, False)
    for block_x in range(count_x):
        for block_y in range(count_y):
            cells = latent_ref[
                block_x * 4 : block_x * 4 + 4, block_y * 4 : block_y * 4 + 4, :, :
            ].reshape(slab, width)
            blocks = jnp.dot(order, cells, preferred_element_type=jnp.float32)
            pad_ref[1 + block_x, 1 + block_y, 1 : 1 + count_z] = (
                blocks.astype(jnp.bfloat16).reshape(count_z, CELLS, width)
            )
    pl.semaphore_wait(barrier, sum(sizes) - 3)

    def has(axis, step):
        return me[axis] > 0 if step < 0 else me[axis] < sizes[axis] - 1

    copies = []

    def layer(axis, side, spans):
        count = counts[axis]
        source = list(spans)
        target = list(spans)
        source[axis] = pl.ds(1 if side < 0 else count, 1)
        target[axis] = pl.ds(count + 1 if side < 0 else 0, 1)
        return tuple(source), tuple(target)

    def send(axis, side, spans, given=None):
        number = len(copies)
        source, target = layer(axis, side, spans)
        to = me[axis] + side
        copy = pltpu.make_async_remote_copy(
            src_ref=pad_ref.at[source],
            dst_ref=pad_ref.at[target],
            send_sem=send_sem.at[number],
            recv_sem=recv_sem.at[number],
            device_id=at(axis, to),
            device_id_type=pl.DeviceIdType.MESH,
        )
        leaves, comes = has(axis, side), has(axis, -side)
        if given is not None:
            leaves, comes = leaves & given, comes & given
        copies.append((copy, leaves, comes))

        @pl.when(leaves)
        def _():
            copy.start()

        return number

    def received(number):
        copy, _, comes = copies[number]

        @pl.when(comes)
        def _():
            copy.wait_recv()

    inner = [pl.ds(1, count) for count in counts]
    sides = (-1, 1)
    face_y = [send(1, side, inner) for side in sides]
    face_z = [send(2, side, inner) for side in sides]
    face_x = [send(0, side, inner) for side in sides]

    cells = latent_ref[...].reshape(-1, width).astype(jnp.float32)
    count = cells.shape[0]
    mean = jnp.sum(cells, axis=0, keepdims=True) / count
    centred = cells - mean
    var = jnp.sum(centred * centred, axis=0, keepdims=True) / count

    first = {0: 0, 1: sizes[0] - 1, 2: sizes[0] + sizes[1] - 2}

    def stat_copies(axis):
        found = []
        for step in range(1, sizes[axis]):
            slot = first[axis] + step - 1
            found.append(
                pltpu.make_async_remote_copy(
                    src_ref=here.at[axis],
                    dst_ref=there.at[slot],
                    send_sem=stat_send.at[slot],
                    recv_sem=stat_recv.at[slot],
                    device_id=at(axis, lax.rem(me[axis] + step, sizes[axis])),
                    device_id_type=pl.DeviceIdType.MESH,
                )
            )
        return found

    def stat_start(axis, mean, var):
        here[axis, 0:1, :] = mean
        here[axis, 1:2, :] = var
        found = stat_copies(axis)
        for copy in found:
            copy.start()
        return found

    def stat_end(axis, found, mean, var):
        for copy in found:
            copy.wait()
        means, variances = [mean], [var]
        for step in range(1, sizes[axis]):
            slot = first[axis] + step - 1
            means.append(there[slot, 0:1, :])
            variances.append(there[slot, 1:2, :])
        mean = sum(means) / sizes[axis]
        spread = [(part - mean) * (part - mean) for part in means]
        return mean, (sum(variances) + sum(spread)) / sizes[axis]

    found = stat_start(0, mean, var)
    mean, var = stat_end(0, found, mean, var)
    found = stat_start(1, mean, var)

    outer_y = [pl.ds(0, 1), pl.ds(count_y + 1, 1)]
    edge_z = []
    for number, side in enumerate(sides):
        received(face_y[1 - number])
        spans = [inner[0], outer_y[number], inner[2]]
        edge_z += [send(2, way, spans, has(1, side)) for way in sides]
    mean, var = stat_end(1, found, mean, var)
    found = stat_start(2, mean, var)
    for number, side in enumerate(sides):
        spans = [inner[0], outer_y[number], inner[2]]
        face_x += [send(0, way, spans, has(1, side)) for way in sides]
    mean, var = stat_end(2, found, mean, var)
    stats_ref[...] = jnp.zeros_like(stats_ref)
    stats_ref[0:1, :] = mean
    stats_ref[1:2, :] = var
    outer_z = [pl.ds(0, 1), pl.ds(count_z + 1, 1)]
    for number, side in enumerate(sides):
        received(face_z[1 - number])
        spans = [inner[0], inner[1], outer_z[number]]
        face_x += [send(0, way, spans, has(2, side)) for way in sides]
    for number, side in enumerate(sides):
        for other, side_y in enumerate(sides):
            received(edge_z[other * 2 + 1 - number])
            spans = [inner[0], outer_y[other], outer_z[number]]
            face_x += [
                send(0, way, spans, has(2, side) & has(1, side_y)) for way in sides
            ]
    for number in face_x:
        received(number)
    for copy, leaves, _ in copies:

        @pl.when(leaves)
        def _(copy=copy):
            copy.wait_send()


def exchange(latent, counts):
    width = latent.shape[-1]
    sizes = tuple(lax.axis_size(axis) for axis in ("gx", "gy", "gz"))
    partners = sum(sizes) - 3
    vmem = pl.BlockSpec(memory_space=pltpu.VMEM)
    padded = tuple(count + 2 for count in counts) + (CELLS, width)
    copies = 2 * (1 + 1 + 1 + 2 + 2 + 2 + 4)
    return pl.pallas_call(
        functools.partial(exchange_kernel, counts, sizes),
        out_shape=(
            jax.ShapeDtypeStruct(padded, jnp.bfloat16),
            jax.ShapeDtypeStruct((8, width), jnp.float32),
        ),
        in_specs=[vmem],
        out_specs=(vmem, vmem),
        scratch_shapes=[
            pltpu.VMEM((3, 8, width), jnp.float32),
            pltpu.VMEM((partners, 8, width), jnp.float32),
            pltpu.SemaphoreType.DMA((copies,)),
            pltpu.SemaphoreType.DMA((copies,)),
            pltpu.SemaphoreType.DMA((partners,)),
            pltpu.SemaphoreType.DMA((partners,)),
        ],
        compiler_params=pltpu.CompilerParams(
            collective_id=0, has_side_effects=True, vmem_limit_bytes=32 * 2**20
        ),
        cost_estimate=pl.CostEstimate(flops=10**9, bytes_accessed=6 * 10**6, transcendentals=0),
    )(latent)


def attend_kernel(
    counts, sizes, limit_ref, x_ref, stats_ref, scale_ref, shift_ref, wqkv_ref, wout_ref,
    bout_ref, out_ref, mean_ref, gain_ref, q_ref, k_ref, v_ref, s_ref, p_ref, mix_ref,
):
    count_x, count_y, count_z = counts
    pad_y, pad_z = count_y + 2, count_z + 2
    width = x_ref.shape[1]
    head_dim = width // HEADS
    keys = CHUNK * CELLS
    factor = head_dim ** (-0.5) * math.log2(math.e)

    per = width // GROUPS
    group = lax.broadcasted_iota(jnp.int32, (width, width), 0) // per
    member = (group == lax.broadcasted_iota(jnp.int32, (width, width), 1) // per).astype(jnp.float32)

    def group_mean(row):
        whole = jnp.broadcast_to(row, (8, width))
        return jnp.dot(
            whole, member, precision=lax.Precision.HIGHEST, preferred_element_type=jnp.float32
        )[0:1] / per

    mean = group_mean(stats_ref[0:1, :])
    apart = stats_ref[0:1, :] - mean
    var = group_mean(stats_ref[1:2, :] + apart * apart)
    mean_ref[...] = mean
    gain_ref[...] = lax.rsqrt(var + 1e-06) * scale_ref[...]

    def normed(x):
        scaled = (x.astype(jnp.float32) - mean_ref[...]) * gain_ref[...]
        return (scaled + shift_ref[...]).astype(jnp.bfloat16)

    place = [lax.axis_index(axis) * n for axis, n in zip(("gx", "gy", "gz"), counts)]

    def low(axis, index):
        return jnp.where(place[axis] + index > 0, index, index + 1)

    def high(axis, index):
        return jnp.where(place[axis] + index + 1 < counts[axis] * sizes[axis], index + 2, index + 1)

    first_x, last_x = low(0, 0), high(0, count_x - 1)
    first_y, last_y = low(1, 0), high(1, count_y - 1)
    column = pad_z * CELLS

    def flat(at_x, at_y, at_z):
        return (at_x * pad_y + at_y) * pad_z + at_z

    def project(index, carry):
        index_x, index_y = index // pad_y, index % pad_y
        inside = (
            (index_x >= first_x) & (index_x <= last_x) & (index_y >= first_y) & (index_y <= last_y)
        )

        @pl.when(inside)
        def _():
            span = pl.ds(pl.multiple_of(index * column, column), column)
            cells = normed(x_ref[span, :])
            k_ref[span, :] = jnp.dot(
                cells, wqkv_ref[:, width : 2 * width], preferred_element_type=jnp.float32
            ).astype(jnp.bfloat16)
            v_ref[span, :] = jnp.dot(
                cells, wqkv_ref[:, 2 * width :], preferred_element_type=jnp.float32
            ).astype(jnp.bfloat16)

        return carry

    lax.fori_loop(0, (count_x + 2) * pad_y, project, 0)

    slab = count_z * CELLS

    def project_query(index, carry):
        source = flat(index // count_y + 1, index % count_y + 1, 1) * CELLS
        cells = normed(x_ref[pl.ds(pl.multiple_of(source, CELLS), slab), :])
        q_ref[pl.ds(pl.multiple_of(index * slab, slab), slab), :] = jnp.dot(
            cells, wqkv_ref[:, :width], preferred_element_type=jnp.float32
        ).astype(jnp.bfloat16)
        return carry

    lax.fori_loop(0, count_x * count_y, project_query, 0)

    half = width // 2
    together = HEADS // 2
    lane_head = lax.broadcasted_iota(jnp.int32, (CELLS, half), 1) // head_dim

    def attend_block(chunks, masked, own, target, start, ends, total):
        lo_x, lo_y, lo_z = start
        hi_x, hi_y, hi_z = ends
        at_x, at_y, at_z = start
        spans = []
        for _ in range(chunks * CHUNK):
            spans.append(pl.ds(pl.multiple_of(flat(at_x, at_y, at_z) * CELLS, CELLS), CELLS))
            turn_z = at_z == hi_z
            at_z = jnp.where(turn_z, lo_z, at_z + 1)
            turn_y = turn_z & (at_y == hi_y)
            at_y = jnp.where(turn_y, lo_y, jnp.where(turn_z, at_y + 1, at_y))
            at_x = jnp.where(turn_y, jnp.minimum(at_x + 1, hi_x), at_x)
        span = pl.ds(pl.multiple_of(own, CELLS), CELLS)
        channels = [slice(group * half, (group + 1) * half) for group in range(2)]
        for group in range(2):
            query = q_ref[span, channels[group]]
            stacked = jnp.concatenate(
                [jnp.where(lane_head == head, query, 0) for head in range(together)], axis=0
            )
            for index in range(chunks):
                chunk = jnp.concatenate(
                    [k_ref[part, channels[group]] for part in spans[index * CHUNK :][:CHUNK]], axis=0
                )
                scores = lax.dot_general(
                    stacked, chunk, (((1,), (1,)), ((), ())), preferred_element_type=jnp.float32
                )
                if index >= masked:
                    lane = lax.broadcasted_iota(jnp.int32, (1, keys), 1) + index * keys
                    scores = jnp.where(lane < total * CELLS, scores, LOW)
                s_ref[group, :, index * keys : (index + 1) * keys] = scores
        for group in range(2):
            shares = []
            for head in range(together):
                rows = slice(head * CELLS, (head + 1) * CELLS)
                scores = s_ref[group, rows, : chunks * keys]
                top = jnp.max(scores, axis=1, keepdims=True) * factor
                weights = jnp.exp2(scores * factor - top)
                shares.append(1.0 / jnp.sum(weights, axis=1, keepdims=True))
                p_ref[group, rows, : chunks * keys] = weights.astype(jnp.bfloat16)
            values = jnp.concatenate([v_ref[part, channels[group]] for part in spans], axis=0)
            summed = jnp.dot(
                p_ref[group, :, : chunks * keys], values, preferred_element_type=jnp.float32
            )
            mixed = jnp.zeros((CELLS, half), jnp.float32)
            for head in range(together):
                rows = slice(head * CELLS, (head + 1) * CELLS)
                mixed = jnp.where(lane_head == head, summed[rows] * shares[head], mixed)
            mix_ref[target, channels[group]] = mixed.astype(jnp.bfloat16)

    forms = ((2, 0), (3, 2), (5, 4), (7, 6))

    def one_block(block_x, block_y, block_z):
        limit = limit_ref[block_x, block_y, block_z]
        lo_x, hi_x = low(0, block_x), high(0, block_x)
        lo_y, hi_y = low(1, block_y), high(1, block_y)
        lo_z = jnp.where(limit > 0, low(2, block_z), block_z + 1)
        hi_z = jnp.where(limit > 0, high(2, block_z), block_z + 1)
        total = (hi_x - lo_x + 1) * (hi_y - lo_y + 1) * (hi_z - lo_z + 1)
        own = ((block_x * count_y + block_y) * count_z + block_z) * CELLS
        target = pl.ds(pl.multiple_of(block_z * CELLS, CELLS), CELLS)
        below = 0
        for chunks, masked in forms:

            @pl.when((total > below * CHUNK) & (total <= chunks * CHUNK))
            def _(chunks=chunks, masked=masked):
                attend_block(
                    chunks, masked, own, target, (lo_x, lo_y, lo_z), (hi_x, hi_y, hi_z), total
                )

            below = chunks

    order = cell_order(slab, True)

    def one_column(index, carry):
        block_x, block_y = index // count_y, index % count_y

        def one_depth(block_z, carry):
            one_block(block_x, block_y, block_z)
            return carry

        lax.fori_loop(0, count_z, one_depth, 0)
        cells = jnp.dot(order, mix_ref[...], preferred_element_type=jnp.float32)
        result = jnp.dot(
            cells.astype(jnp.bfloat16), wout_ref[...], preferred_element_type=jnp.float32
        )
        result = (result + bout_ref[...]).astype(jnp.bfloat16)
        out_ref[pl.ds(block_x * 4, 4), pl.ds(block_y * 4, 4), :, :] = result.reshape(
            4, 4, count_z * 4, width
        )
        return carry

    lax.fori_loop(0, count_x * count_y, one_column, 0)


def attend(limit, padded, stats, gain, shift, w_qkv, w_out, b_out):
    counts = limit.shape
    width = padded.shape[-1]
    flat = padded.reshape(-1, width)
    rows = HEADS * CELLS
    sizes = tuple(lax.axis_size(axis) for axis in ("gx", "gy", "gz"))
    most = -(-27 // CHUNK)
    smem = pl.BlockSpec(memory_space=pltpu.SMEM)
    vmem = pl.BlockSpec(memory_space=pltpu.VMEM)
    return pl.pallas_call(
        functools.partial(attend_kernel, counts, sizes),
        out_shape=jax.ShapeDtypeStruct(
            (counts[0] * 4, counts[1] * 4, counts[2] * 4, width), jnp.bfloat16
        ),
        in_specs=[smem] + [vmem] * 7,
        out_specs=vmem,
        scratch_shapes=[
            pltpu.VMEM((1, width), jnp.float32),
            pltpu.VMEM((1, width), jnp.float32),
            pltpu.VMEM((counts[0] * counts[1] * counts[2] * CELLS, width), jnp.bfloat16),
            pltpu.VMEM(flat.shape, jnp.bfloat16),
            pltpu.VMEM(flat.shape, jnp.bfloat16),
            pltpu.VMEM((2, rows // 2, most * CHUNK * CELLS), jnp.float32),
            pltpu.VMEM((2, rows // 2, most * CHUNK * CELLS), jnp.bfloat16),
            pltpu.VMEM((counts[2] * CELLS, width), jnp.bfloat16),
        ],
        compiler_params=pltpu.CompilerParams(vmem_limit_bytes=48 * 2**20),
        cost_estimate=pl.CostEstimate(
            flops=30 * 10**9, bytes_accessed=7 * 10**6, transcendentals=28 * 10**6
        ),
    )(limit, flat, stats, gain, shift, w_qkv, w_out, b_out)


def on_device(latent, norm_gain, norm_shift, w_qkv, w_out, b_out, depth_limit):
    padded, stats = exchange(latent, depth_limit.shape)
    return attend(
        depth_limit, padded, stats, norm_gain[None], norm_shift[None], w_qkv, w_out, b_out[None]
    )


def solution(mesh):
    placed = (P("gx", "gy", "gz", None), P(), P(), P(), P(), P(), P("gx", "gy", "gz"))
    return jax.shard_map(
        on_device, mesh=mesh, in_specs=placed, out_specs=P("gx", "gy", "gz", None), check_vma=False
    )
```

```python
import functools
import math

import jax
import jax.numpy as jnp
from jax import lax
from jax.experimental import pallas as pl
from jax.experimental.pallas import tpu as pltpu
from jax.sharding import PartitionSpec as P

HEADS = 8
GROUPS = 32
CELLS = 64
CHUNK = 4
LOW = -1e30


def cell_order(slab, inverse):
    natural = lax.broadcasted_iota(jnp.int32, (slab, slab), 0 if inverse else 1)
    blocked = lax.broadcasted_iota(jnp.int32, (slab, slab), 1 if inverse else 0)
    depth = blocked // CELLS * 4 + blocked % 4
    found = blocked % CELLS // 4 * (slab // 16) + depth
    return (found == natural).astype(jnp.bfloat16)


def exchange_kernel(counts, sizes, latent_ref, pad_ref, stats_ref, here, there, *sems):
    send_sem, recv_sem, stat_send, stat_recv = sems
    count_x, count_y, count_z = counts
    width = latent_ref.shape[-1]
    slab = count_z * CELLS
    axes = ("gx", "gy", "gz")
    me = [lax.axis_index(axis) for axis in axes]

    def at(axis, position):
        return tuple(position if n == axis else me[n] for n in range(3))

    barrier = pltpu.get_barrier_semaphore()
    for axis in range(3):
        for step in range(1, sizes[axis]):
            pl.semaphore_signal(
                barrier, inc=1, device_id=at(axis, lax.rem(me[axis] + step, sizes[axis])),
                device_id_type=pl.DeviceIdType.MESH,
            )

    order = cell_order(slab, False)
    for block_x in range(count_x):
        for block_y in range(count_y):
            cells = latent_ref[
                block_x * 4 : block_x * 4 + 4, block_y * 4 : block_y * 4 + 4, :, :
            ].reshape(slab, width)
            blocks = jnp.dot(order, cells, preferred_element_type=jnp.float32)
            pad_ref[1 + block_x, 1 + block_y, 1 : 1 + count_z] = (
                blocks.astype(jnp.bfloat16).reshape(count_z, CELLS, width)
            )
    pl.semaphore_wait(barrier, sum(sizes) - 3)

    def has(axis, step):
        return me[axis] > 0 if step < 0 else me[axis] < sizes[axis] - 1

    copies = []

    def layer(axis, side, spans):
        count = counts[axis]
        source = list(spans)
        target = list(spans)
        source[axis] = pl.ds(1 if side < 0 else count, 1)
        target[axis] = pl.ds(count + 1 if side < 0 else 0, 1)
        return tuple(source), tuple(target)

    def send(axis, side, spans, given=None):
        number = len(copies)
        source, target = layer(axis, side, spans)
        to = me[axis] + side
        copy = pltpu.make_async_remote_copy(
            src_ref=pad_ref.at[source],
            dst_ref=pad_ref.at[target],
            send_sem=send_sem.at[number],
            recv_sem=recv_sem.at[number],
            device_id=at(axis, to),
            device_id_type=pl.DeviceIdType.MESH,
        )
        leaves, comes = has(axis, side), has(axis, -side)
        if given is not None:
            leaves, comes = leaves & given, comes & given
        copies.append((copy, leaves, comes))

        @pl.when(leaves)
        def _():
            copy.start()

        return number

    def received(number):
        copy, _, comes = copies[number]

        @pl.when(comes)
        def _():
            copy.wait_recv()

    inner = [pl.ds(1, count) for count in counts]
    sides = (-1, 1)
    face_y = [send(1, side, inner) for side in sides]
    face_z = [send(2, side, inner) for side in sides]
    face_x = [send(0, side, inner) for side in sides]

    cells = latent_ref[...].reshape(-1, width).astype(jnp.float32)
    count = cells.shape[0]
    mean = jnp.sum(cells, axis=0, keepdims=True) / count
    centred = cells - mean
    var = jnp.sum(centred * centred, axis=0, keepdims=True) / count

    first = {0: 0, 1: sizes[0] - 1, 2: sizes[0] + sizes[1] - 2}

    def stat_copies(axis):
        found = []
        for step in range(1, sizes[axis]):
            slot = first[axis] + step - 1
            found.append(
                pltpu.make_async_remote_copy(
                    src_ref=here.at[axis],
                    dst_ref=there.at[slot],
                    send_sem=stat_send.at[slot],
                    recv_sem=stat_recv.at[slot],
                    device_id=at(axis, lax.rem(me[axis] + step, sizes[axis])),
                    device_id_type=pl.DeviceIdType.MESH,
                )
            )
        return found

    def stat_start(axis, mean, var):
        here[axis, 0:1, :] = mean
        here[axis, 1:2, :] = var
        found = stat_copies(axis)
        for copy in found:
            copy.start()
        return found

    def stat_end(axis, found, mean, var):
        for copy in found:
            copy.wait()
        means, variances = [mean], [var]
        for step in range(1, sizes[axis]):
            slot = first[axis] + step - 1
            means.append(there[slot, 0:1, :])
            variances.append(there[slot, 1:2, :])
        mean = sum(means) / sizes[axis]
        spread = [(part - mean) * (part - mean) for part in means]
        return mean, (sum(variances) + sum(spread)) / sizes[axis]

    found = stat_start(0, mean, var)
    mean, var = stat_end(0, found, mean, var)
    found = stat_start(1, mean, var)

    outer_y = [pl.ds(0, 1), pl.ds(count_y + 1, 1)]
    edge_z = []
    for number, side in enumerate(sides):
        received(face_y[1 - number])
        spans = [inner[0], outer_y[number], inner[2]]
        edge_z += [send(2, way, spans, has(1, side)) for way in sides]
    mean, var = stat_end(1, found, mean, var)
    found = stat_start(2, mean, var)
    for number, side in enumerate(sides):
        spans = [inner[0], outer_y[number], inner[2]]
        face_x += [send(0, way, spans, has(1, side)) for way in sides]
    mean, var = stat_end(2, found, mean, var)
    stats_ref[...] = jnp.zeros_like(stats_ref)
    stats_ref[0:1, :] = mean
    stats_ref[1:2, :] = var
    outer_z = [pl.ds(0, 1), pl.ds(count_z + 1, 1)]
    for number, side in enumerate(sides):
        received(face_z[1 - number])
        spans = [inner[0], inner[1], outer_z[number]]
        face_x += [send(0, way, spans, has(2, side)) for way in sides]
    for number, side in enumerate(sides):
        for other, side_y in enumerate(sides):
            received(edge_z[other * 2 + 1 - number])
            spans = [inner[0], outer_y[other], outer_z[number]]
            face_x += [
                send(0, way, spans, has(2, side) & has(1, side_y)) for way in sides
            ]
    for number in face_x:
        received(number)
    for copy, leaves, _ in copies:

        @pl.when(leaves)
        def _(copy=copy):
            copy.wait_send()


def exchange(latent, counts):
    width = latent.shape[-1]
    sizes = tuple(lax.axis_size(axis) for axis in ("gx", "gy", "gz"))
    partners = sum(sizes) - 3
    vmem = pl.BlockSpec(memory_space=pltpu.VMEM)
    padded = tuple(count + 2 for count in counts) + (CELLS, width)
    copies = 2 * (1 + 1 + 1 + 2 + 2 + 2 + 4)
    return pl.pallas_call(
        functools.partial(exchange_kernel, counts, sizes),
        out_shape=(
            jax.ShapeDtypeStruct(padded, jnp.bfloat16),
            jax.ShapeDtypeStruct((8, width), jnp.float32),
        ),
        in_specs=[vmem],
        out_specs=(vmem, vmem),
        scratch_shapes=[
            pltpu.VMEM((3, 8, width), jnp.float32),
            pltpu.VMEM((partners, 8, width), jnp.float32),
            pltpu.SemaphoreType.DMA((copies,)),
            pltpu.SemaphoreType.DMA((copies,)),
            pltpu.SemaphoreType.DMA((partners,)),
            pltpu.SemaphoreType.DMA((partners,)),
        ],
        compiler_params=pltpu.CompilerParams(
            collective_id=0, has_side_effects=True, vmem_limit_bytes=32 * 2**20
        ),
        cost_estimate=pl.CostEstimate(flops=10**9, bytes_accessed=6 * 10**6, transcendentals=0),
    )(latent)


def attend_kernel(
    counts, sizes, limit_ref, x_ref, stats_ref, scale_ref, shift_ref, wqkv_ref, wout_ref,
    bout_ref, out_ref, mean_ref, gain_ref, q_ref, k_ref, v_ref, s_ref, p_ref, top_ref, mix_ref,
):
    count_x, count_y, count_z = counts
    pad_y, pad_z = count_y + 2, count_z + 2
    width = x_ref.shape[1]
    head_dim = width // HEADS
    keys = CHUNK * CELLS
    factor = head_dim ** (-0.5) * math.log2(math.e)

    per = width // GROUPS
    group = lax.broadcasted_iota(jnp.int32, (width, width), 0) // per
    member = (group == lax.broadcasted_iota(jnp.int32, (width, width), 1) // per).astype(jnp.float32)

    def group_mean(row):
        whole = jnp.broadcast_to(row, (8, width))
        return jnp.dot(
            whole, member, precision=lax.Precision.HIGHEST, preferred_element_type=jnp.float32
        )[0:1] / per

    mean = group_mean(stats_ref[0:1, :])
    apart = stats_ref[0:1, :] - mean
    var = group_mean(stats_ref[1:2, :] + apart * apart)
    mean_ref[...] = mean
    gain_ref[...] = lax.rsqrt(var + 1e-06) * scale_ref[...]

    def normed(x):
        scaled = (x.astype(jnp.float32) - mean_ref[...]) * gain_ref[...]
        return (scaled + shift_ref[...]).astype(jnp.bfloat16)

    place = [lax.axis_index(axis) * n for axis, n in zip(("gx", "gy", "gz"), counts)]

    def low(axis, index):
        return jnp.where(place[axis] + index > 0, index, index + 1)

    def high(axis, index):
        return jnp.where(place[axis] + index + 1 < counts[axis] * sizes[axis], index + 2, index + 1)

    first_x, last_x = low(0, 0), high(0, count_x - 1)
    first_y, last_y = low(1, 0), high(1, count_y - 1)
    column = pad_z * CELLS

    def flat(at_x, at_y, at_z):
        return (at_x * pad_y + at_y) * pad_z + at_z

    def project(index, carry):
        index_x, index_y = index // pad_y, index % pad_y
        inside = (
            (index_x >= first_x) & (index_x <= last_x) & (index_y >= first_y) & (index_y <= last_y)
        )

        @pl.when(inside)
        def _():
            span = pl.ds(pl.multiple_of(index * column, column), column)
            cells = normed(x_ref[span, :])
            k_ref[span, :] = jnp.dot(
                cells, wqkv_ref[:, width : 2 * width], preferred_element_type=jnp.float32
            ).astype(jnp.bfloat16)
            v_ref[span, :] = jnp.dot(
                cells, wqkv_ref[:, 2 * width :], preferred_element_type=jnp.float32
            ).astype(jnp.bfloat16)

        return carry

    lax.fori_loop(0, (count_x + 2) * pad_y, project, 0)

    slab = count_z * CELLS

    def project_query(index, carry):
        source = flat(index // count_y + 1, index % count_y + 1, 1) * CELLS
        cells = normed(x_ref[pl.ds(pl.multiple_of(source, CELLS), slab), :])
        q_ref[pl.ds(pl.multiple_of(index * slab, slab), slab), :] = jnp.dot(
            cells, wqkv_ref[:, :width], preferred_element_type=jnp.float32
        ).astype(jnp.bfloat16)
        return carry

    lax.fori_loop(0, count_x * count_y, project_query, 0)

    half = width // 2
    together = HEADS // 2
    lane_head = lax.broadcasted_iota(jnp.int32, (CELLS, half), 1) // head_dim

    def attend_block(chunks, masked, own, target, start, ends, total):
        lo_x, lo_y, lo_z = start
        hi_x, hi_y, hi_z = ends
        at_x, at_y, at_z = start
        spans = []
        for _ in range(chunks * CHUNK):
            spans.append(pl.ds(pl.multiple_of(flat(at_x, at_y, at_z) * CELLS, CELLS), CELLS))
            turn_z = at_z == hi_z
            at_z = jnp.where(turn_z, lo_z, at_z + 1)
            turn_y = turn_z & (at_y == hi_y)
            at_y = jnp.where(turn_y, lo_y, jnp.where(turn_z, at_y + 1, at_y))
            at_x = jnp.where(turn_y, jnp.minimum(at_x + 1, hi_x), at_x)
        span = pl.ds(pl.multiple_of(own, CELLS), CELLS)
        channels = [slice(group * half, (group + 1) * half) for group in range(2)]
        lanes = [slice(part * 128, (part + 1) * 128) for part in range(chunks * keys // 128)]

        def score(group, stacked, index, best):
            chunk = jnp.concatenate(
                [k_ref[part, channels[group]] for part in spans[index * CHUNK :][:CHUNK]], axis=0
            )
            scores = lax.dot_general(
                stacked, chunk, (((1,), (1,)), ((), ())), preferred_element_type=jnp.float32
            )
            if index >= masked:
                lane = lax.broadcasted_iota(jnp.int32, (1, keys), 1) + index * keys
                scores = jnp.where(lane < total * CELLS, scores, LOW)
            s_ref[group, :, index * keys : (index + 1) * keys] = scores
            for part in range(keys // 128):
                piece = scores[:, part * 128 : (part + 1) * 128]
                best = piece if best is None else jnp.maximum(best, piece)
            return best

        def stack(group):
            query = q_ref[span, channels[group]]
            return jnp.concatenate(
                [jnp.where(lane_head == head, query, 0) for head in range(together)], axis=0
            )

        def keep_top(group, best):
            top = jnp.max(best, axis=1, keepdims=True) * factor
            top_ref[group] = jnp.broadcast_to(top, best.shape)

        def weigh(group, index):
            for lane in lanes[index * (keys // 128) : (index + 1) * (keys // 128)]:
                weights = jnp.exp2(s_ref[group, :, lane] * factor - top_ref[group])
                p_ref[group, :, lane] = weights.astype(jnp.bfloat16)

        def mix(group):
            values = jnp.concatenate([v_ref[part, channels[group]] for part in spans], axis=0)
            summed = jnp.dot(
                p_ref[group, :, : chunks * keys],
                jnp.concatenate([values, jnp.ones_like(values)], axis=1),
                preferred_element_type=jnp.float32,
            )
            mixed = jnp.zeros((CELLS, half), jnp.float32)
            for head in range(together):
                rows = slice(head * CELLS, (head + 1) * CELLS)
                mixed = jnp.where(lane_head == head, summed[rows, :half] / summed[rows, half:], mixed)
            mix_ref[target, channels[group]] = mixed.astype(jnp.bfloat16)

        stacked = stack(0)
        best = None
        for index in range(chunks):
            best = score(0, stacked, index, best)
        keep_top(0, best)
        stacked = stack(1)
        best = None
        for index in range(chunks):
            best = score(1, stacked, index, best)
            weigh(0, index)
        keep_top(1, best)
        mix(0)
        for index in range(chunks):
            weigh(1, index)
        mix(1)

    forms = ((2, 0), (3, 2), (5, 4), (7, 6))

    def one_block(block_x, block_y, block_z):
        limit = limit_ref[block_x, block_y, block_z]
        lo_x, hi_x = low(0, block_x), high(0, block_x)
        lo_y, hi_y = low(1, block_y), high(1, block_y)
        lo_z = jnp.where(limit > 0, low(2, block_z), block_z + 1)
        hi_z = jnp.where(limit > 0, high(2, block_z), block_z + 1)
        total = (hi_x - lo_x + 1) * (hi_y - lo_y + 1) * (hi_z - lo_z + 1)
        own = ((block_x * count_y + block_y) * count_z + block_z) * CELLS
        target = pl.ds(pl.multiple_of(block_z * CELLS, CELLS), CELLS)
        below = 0
        for chunks, masked in forms:

            @pl.when((total > below * CHUNK) & (total <= chunks * CHUNK))
            def _(chunks=chunks, masked=masked):
                attend_block(
                    chunks, masked, own, target, (lo_x, lo_y, lo_z), (hi_x, hi_y, hi_z), total
                )

            below = chunks

    order = cell_order(slab, True)

    def one_column(index, carry):
        block_x, block_y = index // count_y, index % count_y

        def one_depth(block_z, carry):
            one_block(block_x, block_y, block_z)
            return carry

        lax.fori_loop(0, count_z, one_depth, 0)
        cells = jnp.dot(order, mix_ref[...], preferred_element_type=jnp.float32)
        result = jnp.dot(
            cells.astype(jnp.bfloat16), wout_ref[...], preferred_element_type=jnp.float32
        )
        result = (result + bout_ref[...]).astype(jnp.bfloat16)
        out_ref[pl.ds(block_x * 4, 4), pl.ds(block_y * 4, 4), :, :] = result.reshape(
            4, 4, count_z * 4, width
        )
        return carry

    lax.fori_loop(0, count_x * count_y, one_column, 0)


def attend(limit, padded, stats, gain, shift, w_qkv, w_out, b_out):
    counts = limit.shape
    width = padded.shape[-1]
    flat = padded.reshape(-1, width)
    rows = HEADS * CELLS
    sizes = tuple(lax.axis_size(axis) for axis in ("gx", "gy", "gz"))
    most = -(-27 // CHUNK)
    smem = pl.BlockSpec(memory_space=pltpu.SMEM)
    vmem = pl.BlockSpec(memory_space=pltpu.VMEM)
    return pl.pallas_call(
        functools.partial(attend_kernel, counts, sizes),
        out_shape=jax.ShapeDtypeStruct(
            (counts[0] * 4, counts[1] * 4, counts[2] * 4, width), jnp.bfloat16
        ),
        in_specs=[smem] + [vmem] * 7,
        out_specs=vmem,
        scratch_shapes=[
            pltpu.VMEM((1, width), jnp.float32),
            pltpu.VMEM((1, width), jnp.float32),
            pltpu.VMEM((counts[0] * counts[1] * counts[2] * CELLS, width), jnp.bfloat16),
            pltpu.VMEM(flat.shape, jnp.bfloat16),
            pltpu.VMEM(flat.shape, jnp.bfloat16),
            pltpu.VMEM((2, rows // 2, most * CHUNK * CELLS), jnp.float32),
            pltpu.VMEM((2, rows // 2, most * CHUNK * CELLS), jnp.bfloat16),
            pltpu.VMEM((2, rows // 2, 128), jnp.float32),
            pltpu.VMEM((counts[2] * CELLS, width), jnp.bfloat16),
        ],
        compiler_params=pltpu.CompilerParams(vmem_limit_bytes=48 * 2**20),
        cost_estimate=pl.CostEstimate(
            flops=30 * 10**9, bytes_accessed=7 * 10**6, transcendentals=28 * 10**6
        ),
    )(limit, flat, stats, gain, shift, w_qkv, w_out, b_out)


def on_device(latent, norm_gain, norm_shift, w_qkv, w_out, b_out, depth_limit):
    padded, stats = exchange(latent, depth_limit.shape)
    return attend(
        depth_limit, padded, stats, norm_gain[None], norm_shift[None], w_qkv, w_out, b_out[None]
    )


def solution(mesh):
    placed = (P("gx", "gy", "gz", None), P(), P(), P(), P(), P(), P("gx", "gy", "gz"))
    return jax.shard_map(
        on_device, mesh=mesh, in_specs=placed, out_specs=P("gx", "gy", "gz", None), check_vma=False
    )
```

```python
import functools
import math

import jax
import jax.numpy as jnp
from jax import lax
from jax.experimental import pallas as pl
from jax.experimental.pallas import tpu as pltpu
from jax.sharding import PartitionSpec as P

HEADS = 8
GROUPS = 32
CELLS = 64
PIECE = 9


def cell_order(slab, inverse):
    natural = lax.broadcasted_iota(jnp.int32, (slab, slab), 0 if inverse else 1)
    blocked = lax.broadcasted_iota(jnp.int32, (slab, slab), 1 if inverse else 0)
    depth = blocked // CELLS * 4 + blocked % 4
    found = blocked % CELLS // 4 * (slab // 16) + depth
    return (found == natural).astype(jnp.bfloat16)


def exchange_kernel(counts, sizes, latent_ref, pad_ref, stats_ref, here, there, *sems):
    send_sem, recv_sem, stat_send, stat_recv = sems
    count_x, count_y, count_z = counts
    width = latent_ref.shape[-1]
    slab = count_z * CELLS
    axes = ("gx", "gy", "gz")
    me = [lax.axis_index(axis) for axis in axes]

    def at(axis, position):
        return tuple(position if n == axis else me[n] for n in range(3))

    barrier = pltpu.get_barrier_semaphore()
    for axis in range(3):
        for step in range(1, sizes[axis]):
            pl.semaphore_signal(
                barrier, inc=1, device_id=at(axis, lax.rem(me[axis] + step, sizes[axis])),
                device_id_type=pl.DeviceIdType.MESH,
            )

    order = cell_order(slab, False)
    for block_x in range(count_x):
        for block_y in range(count_y):
            cells = latent_ref[
                block_x * 4 : block_x * 4 + 4, block_y * 4 : block_y * 4 + 4, :, :
            ].reshape(slab, width)
            blocks = jnp.dot(order, cells, preferred_element_type=jnp.float32)
            pad_ref[1 + block_x, 1 + block_y, 1 : 1 + count_z] = (
                blocks.astype(jnp.bfloat16).reshape(count_z, CELLS, width)
            )
    pl.semaphore_wait(barrier, sum(sizes) - 3)

    def has(axis, step):
        return me[axis] > 0 if step < 0 else me[axis] < sizes[axis] - 1

    copies = []

    def layer(axis, side, spans):
        count = counts[axis]
        source = list(spans)
        target = list(spans)
        source[axis] = pl.ds(1 if side < 0 else count, 1)
        target[axis] = pl.ds(count + 1 if side < 0 else 0, 1)
        return tuple(source), tuple(target)

    def send(axis, side, spans, given=None):
        number = len(copies)
        source, target = layer(axis, side, spans)
        to = me[axis] + side
        copy = pltpu.make_async_remote_copy(
            src_ref=pad_ref.at[source],
            dst_ref=pad_ref.at[target],
            send_sem=send_sem.at[number],
            recv_sem=recv_sem.at[number],
            device_id=at(axis, to),
            device_id_type=pl.DeviceIdType.MESH,
        )
        leaves, comes = has(axis, side), has(axis, -side)
        if given is not None:
            leaves, comes = leaves & given, comes & given
        copies.append((copy, leaves, comes))

        @pl.when(leaves)
        def _():
            copy.start()

        return number

    def received(number):
        copy, _, comes = copies[number]

        @pl.when(comes)
        def _():
            copy.wait_recv()

    inner = [pl.ds(1, count) for count in counts]
    sides = (-1, 1)
    face_y = [send(1, side, inner) for side in sides]
    face_z = [send(2, side, inner) for side in sides]
    face_x = [send(0, side, inner) for side in sides]

    cells = latent_ref[...].reshape(-1, width).astype(jnp.float32)
    count = cells.shape[0]
    mean = jnp.sum(cells, axis=0, keepdims=True) / count
    centred = cells - mean
    var = jnp.sum(centred * centred, axis=0, keepdims=True) / count

    first = {0: 0, 1: sizes[0] - 1, 2: sizes[0] + sizes[1] - 2}

    def stat_copies(axis):
        found = []
        for step in range(1, sizes[axis]):
            slot = first[axis] + step - 1
            found.append(
                pltpu.make_async_remote_copy(
                    src_ref=here.at[axis],
                    dst_ref=there.at[slot],
                    send_sem=stat_send.at[slot],
                    recv_sem=stat_recv.at[slot],
                    device_id=at(axis, lax.rem(me[axis] + step, sizes[axis])),
                    device_id_type=pl.DeviceIdType.MESH,
                )
            )
        return found

    def stat_start(axis, mean, var):
        here[axis, 0:1, :] = mean
        here[axis, 1:2, :] = var
        found = stat_copies(axis)
        for copy in found:
            copy.start()
        return found

    def stat_end(axis, found, mean, var):
        for copy in found:
            copy.wait()
        means, variances = [mean], [var]
        for step in range(1, sizes[axis]):
            slot = first[axis] + step - 1
            means.append(there[slot, 0:1, :])
            variances.append(there[slot, 1:2, :])
        mean = sum(means) / sizes[axis]
        spread = [(part - mean) * (part - mean) for part in means]
        return mean, (sum(variances) + sum(spread)) / sizes[axis]

    found = stat_start(0, mean, var)
    mean, var = stat_end(0, found, mean, var)
    found = stat_start(1, mean, var)

    outer_y = [pl.ds(0, 1), pl.ds(count_y + 1, 1)]
    edge_z = []
    for number, side in enumerate(sides):
        received(face_y[1 - number])
        spans = [inner[0], outer_y[number], inner[2]]
        edge_z += [send(2, way, spans, has(1, side)) for way in sides]
    mean, var = stat_end(1, found, mean, var)
    found = stat_start(2, mean, var)
    for number, side in enumerate(sides):
        spans = [inner[0], outer_y[number], inner[2]]
        face_x += [send(0, way, spans, has(1, side)) for way in sides]
    mean, var = stat_end(2, found, mean, var)
    stats_ref[...] = jnp.zeros_like(stats_ref)
    stats_ref[0:1, :] = mean
    stats_ref[1:2, :] = var
    outer_z = [pl.ds(0, 1), pl.ds(count_z + 1, 1)]
    for number, side in enumerate(sides):
        received(face_z[1 - number])
        spans = [inner[0], inner[1], outer_z[number]]
        face_x += [send(0, way, spans, has(2, side)) for way in sides]
    for number, side in enumerate(sides):
        for other, side_y in enumerate(sides):
            received(edge_z[other * 2 + 1 - number])
            spans = [inner[0], outer_y[other], outer_z[number]]
            face_x += [
                send(0, way, spans, has(2, side) & has(1, side_y)) for way in sides
            ]
    for number in face_x:
        received(number)
    for copy, leaves, _ in copies:

        @pl.when(leaves)
        def _(copy=copy):
            copy.wait_send()


def exchange(latent, counts):
    width = latent.shape[-1]
    sizes = tuple(lax.axis_size(axis) for axis in ("gx", "gy", "gz"))
    partners = sum(sizes) - 3
    vmem = pl.BlockSpec(memory_space=pltpu.VMEM)
    padded = tuple(count + 2 for count in counts) + (CELLS, width)
    copies = 2 * (1 + 1 + 1 + 2 + 2 + 2 + 4)
    return pl.pallas_call(
        functools.partial(exchange_kernel, counts, sizes),
        out_shape=(
            jax.ShapeDtypeStruct(padded, jnp.bfloat16),
            jax.ShapeDtypeStruct((8, width), jnp.float32),
        ),
        in_specs=[vmem],
        out_specs=(vmem, vmem),
        scratch_shapes=[
            pltpu.VMEM((3, 8, width), jnp.float32),
            pltpu.VMEM((partners, 8, width), jnp.float32),
            pltpu.SemaphoreType.DMA((copies,)),
            pltpu.SemaphoreType.DMA((copies,)),
            pltpu.SemaphoreType.DMA((partners,)),
            pltpu.SemaphoreType.DMA((partners,)),
        ],
        compiler_params=pltpu.CompilerParams(
            collective_id=0, has_side_effects=True, vmem_limit_bytes=32 * 2**20
        ),
        cost_estimate=pl.CostEstimate(flops=10**9, bytes_accessed=6 * 10**6, transcendentals=0),
    )(latent)


def attend_kernel(
    counts, sizes, limit_ref, x_ref, stats_ref, scale_ref, shift_ref, wqkv_ref, wout_ref,
    bout_ref, out_ref, mean_ref, gain_ref, q_ref, k_ref, v_ref, s_ref, p_ref, mix_ref,
):
    count_x, count_y, count_z = counts
    pad_y, pad_z = count_y + 2, count_z + 2
    width = x_ref.shape[1]
    head_dim = width // HEADS
    factor = head_dim ** (-0.5) * math.log2(math.e)

    per = width // GROUPS
    group = lax.broadcasted_iota(jnp.int32, (width, width), 0) // per
    member = (group == lax.broadcasted_iota(jnp.int32, (width, width), 1) // per).astype(jnp.float32)

    def group_mean(row):
        whole = jnp.broadcast_to(row, (8, width))
        return jnp.dot(
            whole, member, precision=lax.Precision.HIGHEST, preferred_element_type=jnp.float32
        )[0:1] / per

    mean = group_mean(stats_ref[0:1, :])
    apart = stats_ref[0:1, :] - mean
    var = group_mean(stats_ref[1:2, :] + apart * apart)
    mean_ref[...] = mean
    gain_ref[...] = lax.rsqrt(var + 1e-06) * scale_ref[...]

    def normed(x):
        scaled = (x.astype(jnp.float32) - mean_ref[...]) * gain_ref[...]
        return (scaled + shift_ref[...]).astype(jnp.bfloat16)

    place = [lax.axis_index(axis) * n for axis, n in zip(("gx", "gy", "gz"), counts)]

    def low(axis, index):
        return jnp.where(place[axis] + index > 0, index, index + 1)

    def high(axis, index):
        return jnp.where(place[axis] + index + 1 < counts[axis] * sizes[axis], index + 2, index + 1)

    first_x, last_x = low(0, 0), high(0, count_x - 1)
    first_y, last_y = low(1, 0), high(1, count_y - 1)
    column = pad_z * CELLS

    def flat(at_x, at_y, at_z):
        return (at_x * pad_y + at_y) * pad_z + at_z

    def project(index, carry):
        index_x, index_y = index // pad_y, index % pad_y
        inside = (
            (index_x >= first_x) & (index_x <= last_x) & (index_y >= first_y) & (index_y <= last_y)
        )

        @pl.when(inside)
        def _():
            span = pl.ds(pl.multiple_of(index * column, column), column)
            cells = normed(x_ref[span, :])
            k_ref[span, :] = jnp.dot(
                cells, wqkv_ref[:, width : 2 * width], preferred_element_type=jnp.float32
            ).astype(jnp.bfloat16)
            v_ref[span, :] = jnp.dot(
                cells, wqkv_ref[:, 2 * width :], preferred_element_type=jnp.float32
            ).astype(jnp.bfloat16)

        return carry

    lax.fori_loop(0, (count_x + 2) * pad_y, project, 0)

    slab = count_z * CELLS

    def project_query(index, carry):
        source = flat(index // count_y + 1, index % count_y + 1, 1) * CELLS
        cells = normed(x_ref[pl.ds(pl.multiple_of(source, CELLS), slab), :])
        q_ref[pl.ds(pl.multiple_of(index * slab, slab), slab), :] = jnp.dot(
            cells, wqkv_ref[:, :width], preferred_element_type=jnp.float32
        ).astype(jnp.bfloat16)
        return carry

    lax.fori_loop(0, count_x * count_y, project_query, 0)

    half = width // 2
    together = HEADS // 2
    lane_head = lax.broadcasted_iota(jnp.int32, (CELLS, half), 1) // head_dim
    stack = together * CELLS
    row_of = lax.broadcasted_iota(jnp.int32, (half, stack), 0) // head_dim
    column_of = lax.broadcasted_iota(jnp.int32, (half, stack), 1) // CELLS
    diagonal = row_of == column_of
    cell = lax.broadcasted_iota(jnp.int32, (CELLS, stack), 0)
    fold = (cell == lax.broadcasted_iota(jnp.int32, (CELLS, stack), 1) % CELLS).astype(jnp.bfloat16)

    def attend_block(blocks, own, target, start, ends):
        lo_x, lo_y, lo_z = start
        hi_x, hi_y, hi_z = ends
        at_x, at_y, at_z = start
        spans = []
        for _ in range(blocks):
            spans.append(pl.ds(pl.multiple_of(flat(at_x, at_y, at_z) * CELLS, CELLS), CELLS))
            turn_z = at_z == hi_z
            at_z = jnp.where(turn_z, lo_z, at_z + 1)
            turn_y = turn_z & (at_y == hi_y)
            at_y = jnp.where(turn_y, lo_y, jnp.where(turn_z, at_y + 1, at_y))
            at_x = jnp.where(turn_y, jnp.minimum(at_x + 1, hi_x), at_x)
        span = pl.ds(pl.multiple_of(own, CELLS), CELLS)
        channels = [slice(group * half, (group + 1) * half) for group in range(2)]
        tops = []
        for group in range(2):
            query = q_ref[span, channels[group]]
            stacked = jnp.concatenate(
                [jnp.where(lane_head == head, query, 0) for head in range(together)], axis=0
            )
            best = None
            for first in range(0, blocks, PIECE):
                part = spans[first : first + PIECE]
                scores = lax.dot_general(
                    jnp.concatenate([k_ref[one, channels[group]] for one in part], axis=0),
                    stacked,
                    (((1,), (1,)), ((), ())),
                    preferred_element_type=jnp.float32,
                )
                s_ref[group, first * CELLS : (first + len(part)) * CELLS, :] = scores
                for one in range(len(part)):
                    piece = scores[one * CELLS : (one + 1) * CELLS]
                    best = piece if best is None else jnp.maximum(best, piece)
            tops.append(jnp.max(best, axis=0, keepdims=True) * factor)
        for group in range(2):
            added = None
            for index in range(blocks):
                rows = slice(index * CELLS, (index + 1) * CELLS)
                weights = jnp.exp2(s_ref[group, rows, :] * factor - tops[group])
                added = weights if added is None else added + weights
                p_ref[group, rows, :] = weights.astype(jnp.bfloat16)
            share = 1.0 / jnp.sum(added, axis=0, keepdims=True)
            values = jnp.concatenate([v_ref[one, channels[group]] for one in spans], axis=0)
            summed = lax.dot_general(
                values,
                p_ref[group, : blocks * CELLS, :],
                (((0,), (0,)), ((), ())),
                preferred_element_type=jnp.float32,
            )
            mixed = jnp.where(diagonal, summed * share, 0.0).astype(jnp.bfloat16)
            mix_ref[target, channels[group]] = lax.dot_general(
                fold, mixed, (((1,), (1,)), ((), ())), preferred_element_type=jnp.float32
            ).astype(jnp.bfloat16)

    forms = sorted({x * y * z for x in (1, 2, 3) for y in (1, 2, 3) for z in (1, 2, 3)})

    def one_block(block_x, block_y, block_z):
        limit = limit_ref[block_x, block_y, block_z]
        lo_x, hi_x = low(0, block_x), high(0, block_x)
        lo_y, hi_y = low(1, block_y), high(1, block_y)
        lo_z = jnp.where(limit > 0, low(2, block_z), block_z + 1)
        hi_z = jnp.where(limit > 0, high(2, block_z), block_z + 1)
        total = (hi_x - lo_x + 1) * (hi_y - lo_y + 1) * (hi_z - lo_z + 1)
        own = ((block_x * count_y + block_y) * count_z + block_z) * CELLS
        target = pl.ds(pl.multiple_of(block_z * CELLS, CELLS), CELLS)
        for blocks in forms:

            @pl.when(total == blocks)
            def _(blocks=blocks):
                attend_block(blocks, own, target, (lo_x, lo_y, lo_z), (hi_x, hi_y, hi_z))

    order = cell_order(slab, True)

    def one_column(index, carry):
        block_x, block_y = index // count_y, index % count_y

        def one_depth(block_z, carry):
            one_block(block_x, block_y, block_z)
            return carry

        lax.fori_loop(0, count_z, one_depth, 0)
        cells = jnp.dot(order, mix_ref[...], preferred_element_type=jnp.float32)
        result = jnp.dot(
            cells.astype(jnp.bfloat16), wout_ref[...], preferred_element_type=jnp.float32
        )
        result = (result + bout_ref[...]).astype(jnp.bfloat16)
        out_ref[pl.ds(block_x * 4, 4), pl.ds(block_y * 4, 4), :, :] = result.reshape(
            4, 4, count_z * 4, width
        )
        return carry

    lax.fori_loop(0, count_x * count_y, one_column, 0)


def attend(limit, padded, stats, gain, shift, w_qkv, w_out, b_out):
    counts = limit.shape
    width = padded.shape[-1]
    flat = padded.reshape(-1, width)
    rows = HEADS * CELLS
    sizes = tuple(lax.axis_size(axis) for axis in ("gx", "gy", "gz"))
    most = 27 * CELLS
    smem = pl.BlockSpec(memory_space=pltpu.SMEM)
    vmem = pl.BlockSpec(memory_space=pltpu.VMEM)
    return pl.pallas_call(
        functools.partial(attend_kernel, counts, sizes),
        out_shape=jax.ShapeDtypeStruct(
            (counts[0] * 4, counts[1] * 4, counts[2] * 4, width), jnp.bfloat16
        ),
        in_specs=[smem] + [vmem] * 7,
        out_specs=vmem,
        scratch_shapes=[
            pltpu.VMEM((1, width), jnp.float32),
            pltpu.VMEM((1, width), jnp.float32),
            pltpu.VMEM((counts[0] * counts[1] * counts[2] * CELLS, width), jnp.bfloat16),
            pltpu.VMEM(flat.shape, jnp.bfloat16),
            pltpu.VMEM(flat.shape, jnp.bfloat16),
            pltpu.VMEM((2, most, rows // 2), jnp.float32),
            pltpu.VMEM((2, most, rows // 2), jnp.bfloat16),
            pltpu.VMEM((counts[2] * CELLS, width), jnp.bfloat16),
        ],
        compiler_params=pltpu.CompilerParams(vmem_limit_bytes=48 * 2**20),
        cost_estimate=pl.CostEstimate(
            flops=30 * 10**9, bytes_accessed=7 * 10**6, transcendentals=28 * 10**6
        ),
    )(limit, flat, stats, gain, shift, w_qkv, w_out, b_out)


def on_device(latent, norm_gain, norm_shift, w_qkv, w_out, b_out, depth_limit):
    padded, stats = exchange(latent, depth_limit.shape)
    return attend(
        depth_limit, padded, stats, norm_gain[None], norm_shift[None], w_qkv, w_out, b_out[None]
    )


def solution(mesh):
    placed = (P("gx", "gy", "gz", None), P(), P(), P(), P(), P(), P("gx", "gy", "gz"))
    return jax.shard_map(
        on_device, mesh=mesh, in_specs=placed, out_specs=P("gx", "gy", "gz", None), check_vma=False
    )
```

```python
import functools
import math

import jax
import jax.numpy as jnp
from jax import lax
from jax.experimental import pallas as pl
from jax.experimental.pallas import tpu as pltpu
from jax.sharding import PartitionSpec as P

HEADS = 8
GROUPS = 32
CELLS = 64
CHUNK = 4
LOW = -1e30


def cell_order(slab, inverse):
    natural = lax.broadcasted_iota(jnp.int32, (slab, slab), 0 if inverse else 1)
    blocked = lax.broadcasted_iota(jnp.int32, (slab, slab), 1 if inverse else 0)
    depth = blocked // CELLS * 4 + blocked % 4
    found = blocked % CELLS // 4 * (slab // 16) + depth
    return (found == natural).astype(jnp.bfloat16)


def exchange_kernel(
    counts, sizes, latent_hbm, scale_hbm, shift_hbm, wqkv_hbm, wout_hbm, bout_hbm, pad_ref, mean_ref,
    gain_ref, shift_ref, wqkv_ref, wout_ref, bout_ref, q_ref, latent_ref, scale_ref, here, there, *sems
):
    send_sem, recv_sem, stat_send, stat_recv, latent_sem, param_sem = sems
    count_x, count_y, count_z = counts
    width = latent_ref.shape[-1]
    slab = count_z * CELLS
    axes = ("gx", "gy", "gz")
    me = [lax.axis_index(axis) for axis in axes]

    def at(axis, position):
        return tuple(position if n == axis else me[n] for n in range(3))

    arriving = []
    for block_x in range(count_x):
        part = pl.ds(block_x * 4, 4)
        arriving.append(
            pltpu.make_async_copy(
                latent_hbm.at[part], latent_ref.at[part], latent_sem.at[block_x]
            )
        )
        arriving[-1].start()
    pairs = (
        (scale_hbm, scale_ref), (shift_hbm, shift_ref), (wqkv_hbm, wqkv_ref),
        (wout_hbm, wout_ref), (bout_hbm, bout_ref),
    )
    params = [
        pltpu.make_async_copy(source, target, param_sem.at[number])
        for number, (source, target) in enumerate(pairs)
    ]
    for copy in params:
        copy.start()

    barrier = pltpu.get_barrier_semaphore()
    for axis in range(3):
        for step in range(1, sizes[axis]):
            pl.semaphore_signal(
                barrier, inc=1, device_id=at(axis, lax.rem(me[axis] + step, sizes[axis])),
                device_id_type=pl.DeviceIdType.MESH,
            )

    order = cell_order(slab, False)
    for block_x in range(count_x):
        arriving[block_x].wait()
        for block_y in range(count_y):
            cells = latent_ref[
                block_x * 4 : block_x * 4 + 4, block_y * 4 : block_y * 4 + 4, :, :
            ].reshape(slab, width)
            blocks = jnp.dot(order, cells, preferred_element_type=jnp.float32)
            pad_ref[1 + block_x, 1 + block_y, 1 : 1 + count_z] = (
                blocks.astype(jnp.bfloat16).reshape(count_z, CELLS, width)
            )
    pl.semaphore_wait(barrier, sum(sizes) - 3)

    def has(axis, step):
        return me[axis] > 0 if step < 0 else me[axis] < sizes[axis] - 1

    copies = []

    def layer(axis, side, spans):
        count = counts[axis]
        source = list(spans)
        target = list(spans)
        source[axis] = pl.ds(1 if side < 0 else count, 1)
        target[axis] = pl.ds(count + 1 if side < 0 else 0, 1)
        return tuple(source), tuple(target)

    def send(axis, side, spans, given=None):
        number = len(copies)
        source, target = layer(axis, side, spans)
        to = me[axis] + side
        copy = pltpu.make_async_remote_copy(
            src_ref=pad_ref.at[source],
            dst_ref=pad_ref.at[target],
            send_sem=send_sem.at[number],
            recv_sem=recv_sem.at[number],
            device_id=at(axis, to),
            device_id_type=pl.DeviceIdType.MESH,
        )
        leaves, comes = has(axis, side), has(axis, -side)
        if given is not None:
            leaves, comes = leaves & given, comes & given
        copies.append((copy, leaves, comes))

        @pl.when(leaves)
        def _():
            copy.start()

        return number

    def received(number):
        copy, _, comes = copies[number]

        @pl.when(comes)
        def _():
            copy.wait_recv()

    inner = [pl.ds(1, count) for count in counts]
    sides = (-1, 1)
    face_y = [send(1, side, inner) for side in sides]
    face_z = [send(2, side, inner) for side in sides]
    face_x = [send(0, side, inner) for side in sides]

    cells = latent_ref[...].reshape(-1, width).astype(jnp.float32)
    count = cells.shape[0]
    mean = jnp.sum(cells, axis=0, keepdims=True) / count
    centred = cells - mean
    var = jnp.sum(centred * centred, axis=0, keepdims=True) / count

    first = {0: 0, 1: sizes[0] - 1, 2: sizes[0] + sizes[1] - 2}

    def stat_copies(axis):
        found = []
        for step in range(1, sizes[axis]):
            slot = first[axis] + step - 1
            found.append(
                pltpu.make_async_remote_copy(
                    src_ref=here.at[axis],
                    dst_ref=there.at[slot],
                    send_sem=stat_send.at[slot],
                    recv_sem=stat_recv.at[slot],
                    device_id=at(axis, lax.rem(me[axis] + step, sizes[axis])),
                    device_id_type=pl.DeviceIdType.MESH,
                )
            )
        return found

    def stat_start(axis, mean, var):
        here[axis, 0:1, :] = mean
        here[axis, 1:2, :] = var
        found = stat_copies(axis)
        for copy in found:
            copy.start()
        return found

    def stat_end(axis, found, mean, var):
        for copy in found:
            copy.wait()
        means, variances = [mean], [var]
        for step in range(1, sizes[axis]):
            slot = first[axis] + step - 1
            means.append(there[slot, 0:1, :])
            variances.append(there[slot, 1:2, :])
        mean = sum(means) / sizes[axis]
        spread = [(part - mean) * (part - mean) for part in means]
        return mean, (sum(variances) + sum(spread)) / sizes[axis]

    found = stat_start(0, mean, var)
    mean, var = stat_end(0, found, mean, var)
    found = stat_start(1, mean, var)

    outer_y = [pl.ds(0, 1), pl.ds(count_y + 1, 1)]
    edge_z = []
    for number, side in enumerate(sides):
        received(face_y[1 - number])
        spans = [inner[0], outer_y[number], inner[2]]
        edge_z += [send(2, way, spans, has(1, side)) for way in sides]
    mean, var = stat_end(1, found, mean, var)
    found = stat_start(2, mean, var)
    for number, side in enumerate(sides):
        spans = [inner[0], outer_y[number], inner[2]]
        face_x += [send(0, way, spans, has(1, side)) for way in sides]
    mean, var = stat_end(2, found, mean, var)
    outer_z = [pl.ds(0, 1), pl.ds(count_z + 1, 1)]
    for number, side in enumerate(sides):
        received(face_z[1 - number])
        spans = [inner[0], inner[1], outer_z[number]]
        face_x += [send(0, way, spans, has(2, side)) for way in sides]
    for number, side in enumerate(sides):
        for other, side_y in enumerate(sides):
            received(edge_z[other * 2 + 1 - number])
            spans = [inner[0], outer_y[other], outer_z[number]]
            face_x += [
                send(0, way, spans, has(2, side) & has(1, side_y)) for way in sides
            ]
    for copy in params:
        copy.wait()
    per = width // GROUPS
    group = lax.broadcasted_iota(jnp.int32, (width, width), 0) // per
    member = (group == lax.broadcasted_iota(jnp.int32, (width, width), 1) // per).astype(jnp.float32)

    def group_mean(row):
        whole = jnp.broadcast_to(row, (8, width))
        return jnp.dot(
            whole, member, precision=lax.Precision.HIGHEST, preferred_element_type=jnp.float32
        )[0:1] / per

    centre = group_mean(mean)
    var = group_mean(var + (mean - centre) * (mean - centre))
    mean_ref[...] = centre
    gain_ref[...] = lax.rsqrt(var + 1e-06) * scale_ref[...]
    for block_x in range(count_x):
        for block_y in range(count_y):
            cells = pad_ref[1 + block_x, 1 + block_y, 1 : 1 + count_z].reshape(slab, width)
            scaled = (cells.astype(jnp.float32) - mean_ref[...]) * gain_ref[...] + shift_ref[...]
            q_ref[pl.ds((block_x * count_y + block_y) * slab, slab), :] = jnp.dot(
                scaled.astype(jnp.bfloat16), wqkv_ref[:, :width],
                preferred_element_type=jnp.float32,
            ).astype(jnp.bfloat16)
    for number in face_x:
        received(number)
    for copy, leaves, _ in copies:

        @pl.when(leaves)
        def _(copy=copy):
            copy.wait_send()


def exchange(latent, counts, gain, shift, w_qkv, w_out, b_out):
    width = latent.shape[-1]
    sizes = tuple(lax.axis_size(axis) for axis in ("gx", "gy", "gz"))
    partners = sum(sizes) - 3
    vmem = pl.BlockSpec(memory_space=pltpu.VMEM)
    padded = tuple(count + 2 for count in counts) + (CELLS, width)
    copies = 2 * (1 + 1 + 1 + 2 + 2 + 2 + 4)
    return pl.pallas_call(
        functools.partial(exchange_kernel, counts, sizes),
        out_shape=(
            jax.ShapeDtypeStruct(padded, jnp.bfloat16),
            jax.ShapeDtypeStruct((1, width), jnp.float32),
            jax.ShapeDtypeStruct((1, width), jnp.float32),
            jax.ShapeDtypeStruct((1, width), jnp.float32),
            jax.ShapeDtypeStruct(w_qkv.shape, jnp.bfloat16),
            jax.ShapeDtypeStruct(w_out.shape, jnp.bfloat16),
            jax.ShapeDtypeStruct((1, width), jnp.float32),
            jax.ShapeDtypeStruct((math.prod(counts) * CELLS, width), jnp.bfloat16),
        ),
        in_specs=[pl.BlockSpec(memory_space=pltpu.HBM)] * 6,
        out_specs=(vmem,) * 8,
        scratch_shapes=[
            pltpu.VMEM(latent.shape, jnp.bfloat16),
            pltpu.VMEM((1, width), jnp.float32),
            pltpu.VMEM((3, 8, width), jnp.float32),
            pltpu.VMEM((partners, 8, width), jnp.float32),
            pltpu.SemaphoreType.DMA((copies,)),
            pltpu.SemaphoreType.DMA((copies,)),
            pltpu.SemaphoreType.DMA((partners,)),
            pltpu.SemaphoreType.DMA((partners,)),
            pltpu.SemaphoreType.DMA((counts[0],)),
            pltpu.SemaphoreType.DMA((5,)),
        ],
        compiler_params=pltpu.CompilerParams(
            collective_id=0, has_side_effects=True, vmem_limit_bytes=58 * 2**20
        ),
        cost_estimate=pl.CostEstimate(flops=10**9, bytes_accessed=6 * 10**6, transcendentals=0),
    )(latent, gain, shift, w_qkv, w_out, b_out)


def attend_kernel(
    counts, sizes, limit_ref, x_ref, mean_ref, gain_ref, shift_ref, wqkv_ref, wout_ref,
    bout_ref, q_ref, out_ref, k_ref, v_ref, s_ref, p_ref, mix_ref,
):
    count_x, count_y, count_z = counts
    pad_y, pad_z = count_y + 2, count_z + 2
    width = x_ref.shape[1]
    head_dim = width // HEADS
    keys = CHUNK * CELLS
    factor = head_dim ** (-0.5) * math.log2(math.e)

    def normed(x):
        scaled = (x.astype(jnp.float32) - mean_ref[...]) * gain_ref[...]
        return (scaled + shift_ref[...]).astype(jnp.bfloat16)

    place = [lax.axis_index(axis) * n for axis, n in zip(("gx", "gy", "gz"), counts)]

    def low(axis, index):
        return jnp.where(place[axis] + index > 0, index, index + 1)

    def high(axis, index):
        return jnp.where(place[axis] + index + 1 < counts[axis] * sizes[axis], index + 2, index + 1)

    first_x, last_x = low(0, 0), high(0, count_x - 1)
    first_y, last_y = low(1, 0), high(1, count_y - 1)
    column = pad_z * CELLS

    def flat(at_x, at_y, at_z):
        return (at_x * pad_y + at_y) * pad_z + at_z

    def project(index, carry):
        index_x, index_y = index // pad_y, index % pad_y
        inside = (
            (index_x >= first_x) & (index_x <= last_x) & (index_y >= first_y) & (index_y <= last_y)
        )

        @pl.when(inside)
        def _():
            span = pl.ds(pl.multiple_of(index * column, column), column)
            cells = normed(x_ref[span, :])
            k_ref[span, :] = jnp.dot(
                cells, wqkv_ref[:, width : 2 * width], preferred_element_type=jnp.float32
            ).astype(jnp.bfloat16)
            v_ref[span, :] = jnp.dot(
                cells, wqkv_ref[:, 2 * width :], preferred_element_type=jnp.float32
            ).astype(jnp.bfloat16)

        return carry

    lax.fori_loop(0, (count_x + 2) * pad_y, project, 0)

    slab = count_z * CELLS

    half = width // 2
    together = HEADS // 2
    lane_head = lax.broadcasted_iota(jnp.int32, (CELLS, half), 1) // head_dim

    def attend_block(chunks, masked, own, target, start, ends, total):
        lo_x, lo_y, lo_z = start
        hi_x, hi_y, hi_z = ends
        at_x, at_y, at_z = start
        spans = []
        for _ in range(chunks * CHUNK):
            spans.append(pl.ds(pl.multiple_of(flat(at_x, at_y, at_z) * CELLS, CELLS), CELLS))
            turn_z = at_z == hi_z
            at_z = jnp.where(turn_z, lo_z, at_z + 1)
            turn_y = turn_z & (at_y == hi_y)
            at_y = jnp.where(turn_y, lo_y, jnp.where(turn_z, at_y + 1, at_y))
            at_x = jnp.where(turn_y, jnp.minimum(at_x + 1, hi_x), at_x)
        span = pl.ds(pl.multiple_of(own, CELLS), CELLS)
        channels = [slice(group * half, (group + 1) * half) for group in range(2)]
        for group in range(2):
            query = q_ref[span, channels[group]]
            stacked = jnp.concatenate(
                [jnp.where(lane_head == head, query, 0) for head in range(together)], axis=0
            )
            for index in range(chunks):
                chunk = jnp.concatenate(
                    [k_ref[part, channels[group]] for part in spans[index * CHUNK :][:CHUNK]], axis=0
                )
                scores = lax.dot_general(
                    stacked, chunk, (((1,), (1,)), ((), ())), preferred_element_type=jnp.float32
                )
                if index >= masked:
                    lane = lax.broadcasted_iota(jnp.int32, (1, keys), 1) + index * keys
                    scores = jnp.where(lane < total * CELLS, scores, LOW)
                s_ref[group, :, index * keys : (index + 1) * keys] = scores
        for group in range(2):
            shares = []
            for head in range(together):
                rows = slice(head * CELLS, (head + 1) * CELLS)
                scores = s_ref[group, rows, : chunks * keys]
                top = jnp.max(scores, axis=1, keepdims=True) * factor
                weights = jnp.exp2(scores * factor - top)
                shares.append(1.0 / jnp.sum(weights, axis=1, keepdims=True))
                p_ref[group, rows, : chunks * keys] = weights.astype(jnp.bfloat16)
            values = jnp.concatenate([v_ref[part, channels[group]] for part in spans], axis=0)
            summed = jnp.dot(
                p_ref[group, :, : chunks * keys], values, preferred_element_type=jnp.float32
            )
            mixed = jnp.zeros((CELLS, half), jnp.float32)
            for head in range(together):
                rows = slice(head * CELLS, (head + 1) * CELLS)
                mixed = jnp.where(lane_head == head, summed[rows] * shares[head], mixed)
            mix_ref[target, channels[group]] = mixed.astype(jnp.bfloat16)

    forms = ((2, 0), (3, 2), (5, 4), (7, 6))

    def one_block(block_x, block_y, block_z):
        limit = limit_ref[block_x, block_y, block_z]
        lo_x, hi_x = low(0, block_x), high(0, block_x)
        lo_y, hi_y = low(1, block_y), high(1, block_y)
        lo_z = jnp.where(limit > 0, low(2, block_z), block_z + 1)
        hi_z = jnp.where(limit > 0, high(2, block_z), block_z + 1)
        total = (hi_x - lo_x + 1) * (hi_y - lo_y + 1) * (hi_z - lo_z + 1)
        own = ((block_x * count_y + block_y) * count_z + block_z) * CELLS
        target = pl.ds(pl.multiple_of(block_z * CELLS, CELLS), CELLS)
        below = 0
        for chunks, masked in forms:

            @pl.when((total > below * CHUNK) & (total <= chunks * CHUNK))
            def _(chunks=chunks, masked=masked):
                attend_block(
                    chunks, masked, own, target, (lo_x, lo_y, lo_z), (hi_x, hi_y, hi_z), total
                )

            below = chunks

    order = cell_order(slab, True)

    def one_column(index, carry):
        block_x, block_y = index // count_y, index % count_y

        def one_depth(block_z, carry):
            one_block(block_x, block_y, block_z)
            return carry

        lax.fori_loop(0, count_z, one_depth, 0)
        cells = jnp.dot(order, mix_ref[...], preferred_element_type=jnp.float32)
        result = jnp.dot(
            cells.astype(jnp.bfloat16), wout_ref[...], preferred_element_type=jnp.float32
        )
        result = (result + bout_ref[...]).astype(jnp.bfloat16)
        out_ref[pl.ds(block_x * 4, 4), pl.ds(block_y * 4, 4), :, :] = result.reshape(
            4, 4, count_z * 4, width
        )
        return carry

    lax.fori_loop(0, count_x * count_y, one_column, 0)


def attend(limit, padded, mean, gain, shift, w_qkv, w_out, b_out, queries):
    counts = limit.shape
    width = padded.shape[-1]
    flat = padded.reshape(-1, width)
    rows = HEADS * CELLS
    sizes = tuple(lax.axis_size(axis) for axis in ("gx", "gy", "gz"))
    most = -(-27 // CHUNK)
    smem = pl.BlockSpec(memory_space=pltpu.SMEM)
    vmem = pl.BlockSpec(memory_space=pltpu.VMEM)
    return pl.pallas_call(
        functools.partial(attend_kernel, counts, sizes),
        out_shape=jax.ShapeDtypeStruct(
            (counts[0] * 4, counts[1] * 4, counts[2] * 4, width), jnp.bfloat16
        ),
        in_specs=[smem] + [vmem] * 8,
        out_specs=vmem,
        scratch_shapes=[
            pltpu.VMEM(flat.shape, jnp.bfloat16),
            pltpu.VMEM(flat.shape, jnp.bfloat16),
            pltpu.VMEM((2, rows // 2, most * CHUNK * CELLS), jnp.float32),
            pltpu.VMEM((2, rows // 2, most * CHUNK * CELLS), jnp.bfloat16),
            pltpu.VMEM((counts[2] * CELLS, width), jnp.bfloat16),
        ],
        compiler_params=pltpu.CompilerParams(vmem_limit_bytes=58 * 2**20),
        cost_estimate=pl.CostEstimate(
            flops=30 * 10**9, bytes_accessed=7 * 10**6, transcendentals=28 * 10**6
        ),
    )(limit, flat, mean, gain, shift, w_qkv, w_out, b_out, queries)


def on_device(latent, norm_gain, norm_shift, w_qkv, w_out, b_out, depth_limit):
    return attend(
        depth_limit,
        *exchange(
            latent, depth_limit.shape, norm_gain[None], norm_shift[None], w_qkv, w_out, b_out[None]
        ),
    )


def solution(mesh):
    placed = (P("gx", "gy", "gz", None), P(), P(), P(), P(), P(), P("gx", "gy", "gz"))
    return jax.shard_map(
        on_device, mesh=mesh, in_specs=placed, out_specs=P("gx", "gy", "gz", None), check_vma=False
    )
```
